512 devices in a mesh: node: 32 (over y, z_lo), hst: 8 (over x, core), dp: 2 (over z_hi).
Axes of the slice: x: 4, y: 8, z: 8 (z_hi: 2, z_lo: 4; z = z_hi * 4 + z_lo), core: 2. Of those that a mesh axis runs over, the one named last changes fastest.
Arguments:
- partials: bfloat16 [8, 4096, 128, 192], P('hst', 'dp', 'node'), may hold values from -6 to 6
- counts: int32 [2, 8, 256, 128], P('dp', 'hst', 'node'), may hold values from 0 to 5
- perm: int32 [128], replicated, may hold values from 0 to 127, each once
- fm_proj: bfloat16 [128, 32], replicated, may hold values from -0.5 to 0.5
- ln_gain: float32 [4096], replicated, may hold values from 0.1 to 1.9
- w_in: bfloat16 [4096, 4096], P('hst', 'node'), may hold values from -0.09375 to 0.09375
- d_hidden: bfloat16 [2, 8, 256, 4096], P('dp', 'hst', None, 'node'), may hold values from -0.5 to 0.5
Outputs:
- hidden: bfloat16 [2, 8, 256, 4096], P('dp', 'hst', None, 'node')
- grad_w: float32 [4096, 4096], P('hst', 'node')
The draws below stay inside these ranges and needn't reach their ends.
Inputs may be any that keep to these rules, and one draw needn't show every extreme that they name: perm names each of the 128 features once.
All inputs are finite; a program needn't handle non-finite values.
Results may differ from the reference program's by a relative error of at most 0.03.
Values may be sent and summed in bfloat16 or wider, within the bound.
No kernel may reach another device: no remote copies, remote signals or barrier semaphores. Data moves between devices by JAX's collectives and lax.ppermute only.
A program may use at most 64 MiB of HBM per device.

```python
import jax
import jax.numpy as jnp
from jax import lax

F = 128
E = 192
K = 32
H = 4096
FK = 4096
GROUP = 256
BATCH = 4096
N_HST = 8
N_DP = 2


def place_ends(result, stream_key, low, top_value):
    dims = result.shape
    index_at = [jax.random.randint(jax.random.fold_in(stream_key, axis), (), 0, dims[axis]) for axis in range(len(dims))]
    result = result.at[tuple(index_at)].set(low)
    longest = dims.index(max(dims))
    index_at[longest] = (index_at[longest] + 1) % dims[longest]
    return result.at[tuple(index_at)].set(top_value)


def strengthened(values, own_key, source, target, shards_of, factor):
    owner, partner = [(jnp.arange(values.shape[dim]) // (values.shape[dim] // shards_of)).reshape([-1 if axis == dim else 1 for axis in range(values.ndim)]) for dim in (source, target)]
    chosen = jax.random.permutation(own_key, shards_of)[partner]
    strong = (owner == chosen) | (owner == (partner + shards_of // 2) % shards_of)
    return jnp.where(strong, factor * values, values)


def block_scale(key, dims, cuts, least, top_value):
    loudness = 1.0
    for dim, shards_of in cuts:
        steps = jax.random.uniform(jax.random.fold_in(jax.random.fold_in(key, 6), dim), (shards_of,), jnp.float32, least / len(cuts), top_value / len(cuts))
        loudness = loudness * jnp.repeat(jnp.exp(steps), dims[dim] // shards_of).reshape((-1,) + (1,) * (len(dims) - 1 - dim))
    return loudness


def normal_values(own_key, shape, scale, reach, split=(), held_as=jnp.bfloat16):
    drawn = scale * jax.random.normal(own_key, shape, jnp.float32)
    if split:
        drawn = drawn * block_scale(own_key, shape, split, -0.22, 0.18)
    return jnp.clip(drawn, -reach, reach).astype(held_as)


def noise_with(rng, dims, width, reach, cuts, heavy, held_as=jnp.bfloat16):
    entries = width * jax.random.normal(rng, dims, jnp.float32)
    if cuts:
        entries = entries * block_scale(rng, dims, cuts, -0.22, 0.18)
    return jnp.clip(strengthened(entries, jax.random.fold_in(rng, 3), *heavy), -reach, reach).astype(held_as)


def setup_inputs(seed: int = 0) -> dict:
    streams_of = jax.random.split(jax.random.key(seed), 8)
    return {
        "partials": noise_with(streams_of[0], (N_HST, BATCH, F, E), 1.0, 6.0, ((0, 8), (1, 2), (2, 32)), (0, 1, 8, 2.0)),
        "counts": place_ends(jax.random.randint(streams_of[1], (N_DP, N_HST, GROUP, F), 0, 6), jax.random.fold_in(streams_of[1], 1), 0, 5).astype(jnp.int32),
        "perm": jax.random.permutation(streams_of[2], F).astype(jnp.int32),
        "fm_proj": normal_values(streams_of[3], (F, K), F ** -0.5, 0.5),
        "ln_gain": jnp.clip(1.0 + 0.18 * jax.random.normal(streams_of[4], (FK,), jnp.float32), 0.1, 1.9),
        "w_in": normal_values(streams_of[5], (FK, H), FK ** -0.5, 0.09375, ((0, 8), (1, 32))),
        "d_hidden": normal_values(streams_of[6], (N_DP, N_HST, GROUP, H), (2.0 / BATCH ** 0.5), 0.5, ((0, 2), (1, 8), (3, 32))),
    }


def normalize(flat_rows, ln_gain):
    middle = lax.optimization_barrier(jnp.mean(flat_rows, axis=-1, keepdims=True))
    centered = flat_rows - middle
    variance = lax.optimization_barrier(jnp.mean(centered * centered, axis=-1, keepdims=True))
    return (centered * lax.rsqrt(variance + 1e-05) * ln_gain).astype(jnp.bfloat16)

def reference(partials, counts, perm, fm_proj, ln_gain, w_in, d_hidden):

    def add_shard(total, piece):
        return (total + piece.astype(jnp.float32), None)
    start_sum = jnp.zeros(partials.shape[1:], jnp.float32)
    summed, unused = lax.scan(add_shard, start_sum, partials)
    summed = summed.astype(jnp.bfloat16)
    ordered = jnp.take(summed, perm, axis=1)
    count_rows = counts.reshape(BATCH, F)
    divisor = jnp.maximum(count_rows, 1).astype(jnp.float32)[:, :, None]
    pooled = jnp.where(count_rows[:, :, None] > 0, ordered.astype(jnp.float32) / divisor, 0.0).astype(jnp.bfloat16)
    groups = N_DP * N_HST
    pooled_groups = pooled.reshape(groups, GROUP, F, E)
    cot_groups = d_hidden.reshape(groups, GROUP, H)

    def one_group(total, items):
        pooled_here, cot_here = items
        proj = jnp.einsum('sfe,fk->sek', pooled_here.astype(jnp.float32), fm_proj.astype(jnp.float32)).astype(jnp.bfloat16)
        inter = jnp.einsum('sfe,sek->sfk', pooled_here.astype(jnp.float32), proj.astype(jnp.float32))
        z_rows = normalize(inter.reshape(GROUP, FK), ln_gain)
        pre_act = jnp.dot(z_rows, w_in, preferred_element_type=jnp.float32)
        sigma = jax.nn.sigmoid(pre_act)
        hidden_here = (pre_act * sigma).astype(jnp.bfloat16)
        d_pre = (cot_here.astype(jnp.float32) * sigma * (1.0 + pre_act * (1.0 - sigma))).astype(jnp.bfloat16)
        term = lax.dot_general(z_rows, d_pre, (((0,), (0,)), ((), ())), preferred_element_type=jnp.float32)
        term = lax.optimization_barrier(term.astype(jnp.bfloat16)).astype(jnp.float32)
        return (total + term, hidden_here)
    start_grad = jnp.zeros((FK, H), jnp.float32)
    grad_w, hidden = lax.scan(one_group, start_grad, (pooled_groups, cot_groups))
    return (hidden.reshape(N_DP, N_HST, GROUP, H), grad_w)
```

```python
import jax
import jax.numpy as jnp
from jax import lax
from jax.sharding import PartitionSpec as P

N_X = 4
N_CORE = 2
N_Y = 8
N_Z = 4

CORE_SWAP = [(h, h ^ 1) for h in range(N_X * N_CORE)]
X_UP = [(2 * x + c, 2 * ((x + 1) % N_X) + c) for x in range(N_X) for c in range(N_CORE)]
X_DOWN = [(b, a) for a, b in X_UP]
Y_UP = [(N_Z * y + z, N_Z * ((y + 1) % N_Y) + z) for y in range(N_Y) for z in range(N_Z)]
Y_DOWN = [(b, a) for a, b in Y_UP]
DP_SWAP = [(0, 1), (1, 0)]


def z_shift(k):
    return [(N_Z * y + z, N_Z * y + (z + k) % N_Z) for y in range(N_Y) for z in range(N_Z)]


def add(*terms):
    total = terms[0].astype(jnp.float32)
    for term in terms[1:]:
        total = total + term.astype(jnp.float32)
    return total


def pick(pieces, index):
    return lax.dynamic_index_in_dim(pieces, index, 0, keepdims=False)


def scatter_sum(pieces):
    h = lax.axis_index("hst")
    x, c = h // N_CORE, h % N_CORE
    given = lax.dynamic_index_in_dim(pieces, 1 - c, 1, keepdims=False)
    kept = lax.dynamic_index_in_dim(pieces, c, 1, keepdims=False)
    got = lax.ppermute(given, "hst", CORE_SWAP)
    pair = add(kept, got).astype(jnp.bfloat16)
    half = pair.shape[1] // 2
    far = pick(pair, (x + 2) % N_X)
    up, down = pick(pair, (x + 1) % N_X), pick(pair, (x + 3) % N_X)
    own = pick(pair, x)
    far_up = lax.ppermute(far[:half], "hst", X_UP)
    far_down = lax.ppermute(far[half:], "hst", X_DOWN)
    up_b = lax.ppermute(up[half:], "hst", X_UP)
    down_a = lax.ppermute(down[:half], "hst", X_DOWN)
    up_a = lax.ppermute(add(up[:half], far_up).astype(jnp.bfloat16), "hst", X_UP)
    down_b = lax.ppermute(add(down[half:], far_down).astype(jnp.bfloat16), "hst", X_DOWN)
    return jnp.concatenate([add(own[:half], up_a, down_a), add(own[half:], up_b, down_b)], 0)


def normalize(flat_rows, ln_gain):
    middle = jnp.mean(flat_rows, axis=-1, keepdims=True)
    centered = flat_rows - middle
    variance = jnp.mean(centered * centered, axis=-1, keepdims=True)
    return (centered * lax.rsqrt(variance + 1e-05) * ln_gain).astype(jnp.bfloat16)


def gather_nodes(block):
    near = [block] + [lax.ppermute(block, "node", z_shift(k)) for k in range(1, N_Z)]
    line = jnp.concatenate(near, 0)
    half = line.shape[0] // 2
    ups, downs = [line], [line]
    for _ in range(3):
        ups.append(lax.ppermute(ups[-1], "node", Y_UP))
        downs.append(lax.ppermute(downs[-1], "node", Y_DOWN))
    far_a = lax.ppermute(ups[-1][:half], "node", Y_UP)
    far_b = lax.ppermute(downs[-1][half:], "node", Y_DOWN)
    return jnp.concatenate(ups + [far_a, far_b] + downs[:0:-1], 0)


def local(partials, counts, perm, fm_proj, ln_gain, w_in, d_hidden):
    samples = counts.shape[2]
    group, hidden_here = d_hidden.shape[2], d_hidden.shape[3]
    w_full = lax.all_gather(w_in, "hst", axis=0, tiled=True)

    n = lax.axis_index("node")
    y, z = n // N_Z, n % N_Z
    steps = jnp.arange(N_Y * N_Z)
    order = ((y - steps // N_Z) % N_Y) * N_Z + (z - steps % N_Z) % N_Z
    d_hid = jnp.take(d_hidden[0, 0].reshape(N_Y * N_Z, samples, hidden_here), order, axis=0)
    d_hid = d_hid.reshape(group, hidden_here)

    rows = partials.shape[2] * partials.shape[3]
    flat = partials[0].transpose(1, 2, 0).reshape(rows, N_X, N_CORE, group).transpose(1, 2, 0, 3)
    summed = scatter_sum(flat).astype(jnp.bfloat16).T
    shard_rows = lax.all_to_all(
        summed.reshape(N_Y * N_Z, samples, rows), "node", split_axis=0, concat_axis=0, tiled=True
    )
    shard_rows = shard_rows.transpose(1, 0, 2).reshape(samples, -1, partials.shape[3])
    ordered = jnp.take(shard_rows, perm, axis=1)
    counts_here = counts[0, 0]
    divisor = jnp.maximum(counts_here, 1).astype(jnp.float32)[:, :, None]
    pooled = jnp.where(
        counts_here[:, :, None] > 0, ordered.astype(jnp.float32) / divisor, 0.0
    ).astype(jnp.bfloat16)
    projected = jnp.einsum(
        "sfe,fk->sek", pooled, fm_proj, preferred_element_type=jnp.float32
    ).astype(jnp.bfloat16)
    pairwise = jnp.einsum("sfe,sek->sfk", pooled, projected, preferred_element_type=jnp.float32)
    z_local = normalize(pairwise.reshape(samples, -1), ln_gain)

    z_group = gather_nodes(z_local)
    pre_act = jnp.dot(z_group, w_full, preferred_element_type=jnp.float32)
    sigma = jax.nn.sigmoid(pre_act)
    hidden = (pre_act * sigma).astype(jnp.bfloat16)
    hidden = jnp.take(hidden.reshape(N_Y * N_Z, samples, hidden_here), order, axis=0)
    d_pre = (d_hid.astype(jnp.float32) * sigma * (1.0 + pre_act * (1.0 - sigma))).astype(
        jnp.bfloat16
    )
    term = lax.dot_general(
        z_group, d_pre, (((0,), (0,)), ((), ())), preferred_element_type=jnp.float32
    ).astype(jnp.bfloat16)
    share = scatter_sum(term.reshape(N_X, N_CORE, w_in.shape[0], hidden_here)).astype(jnp.bfloat16)
    other = lax.ppermute(share, "dp", DP_SWAP)
    grad_w = add(share, other)
    return (hidden.reshape(1, 1, group, hidden_here), grad_w)


def solution(mesh):
    in_specs = (
        P("hst", "dp", "node", None),
        P("dp", "hst", "node", None),
        P(),
        P(),
        P(),
        P("hst", "node"),
        P("dp", "hst", None, "node"),
    )
    out_specs = (P("dp", "hst", None, "node"), P("hst", "node"))
    return jax.shard_map(local, mesh=mesh, in_specs=in_specs, out_specs=out_specs, check_vma=False)
```

```python
import jax
import jax.numpy as jnp
from jax import lax
from jax.experimental import pallas as pl
from jax.experimental.pallas import tpu as pltpu
from jax.sharding import PartitionSpec as P

N_X = 4
N_CORE = 2
N_Y = 8
N_Z = 4
VMEM = 12 * 2**20

def swaps(size, partner):
    return [(i, partner(i)) for i in range(size)]


CORE_SWAP = swaps(N_X * N_CORE, lambda h: h ^ 1)
X_EVEN = swaps(N_X * N_CORE, lambda h: h ^ 2)
X_ODD = swaps(N_X * N_CORE, lambda h: h ^ 6)
Z_NEAR = swaps(N_Y * N_Z, lambda n: n ^ 1)
Z_FAR = swaps(N_Y * N_Z, lambda n: n ^ 2)
Y_EVEN = swaps(N_Y * N_Z, lambda n: n ^ N_Z)
Y_ODD = swaps(N_Y * N_Z, lambda n: (((n // N_Z + 1) ^ 1) - 1) % N_Y * N_Z + n % N_Z)
DP_SWAP = swaps(2, lambda d: d ^ 1)
Y_DISTANCE = (0, 1, -1, 2, -2, 3, -3, 4)
Y_SLOT = (0, 1, 3, 5, 7, 6, 4, 2)


def add(*terms):
    total = terms[0].astype(jnp.float32)
    for term in terms[1:]:
        total = total + term.astype(jnp.float32)
    return total


def pack_kernel(columns_ref, rows_ref, out_ref):
    out_ref[...] = rows_ref[...]


def pair_kernel(columns_ref, rows_ref, got_ref, a_keep, a_send, b_keep, b_send):
    step = pl.program_id(0)
    total = add(rows_ref[...], got_ref[...]).astype(a_keep.dtype)
    half = total.shape[0] // 2

    @pl.when(step <= 1)
    def _():
        a_keep[0] = total[:half]

    @pl.when(step >= 2)
    def _():
        a_send[0] = total[:half]

    @pl.when(step % 2 == 0)
    def _():
        b_keep[0] = total[half:]

    @pl.when(step % 2 == 1)
    def _():
        b_send[0] = total[half:]


def turn_kernel(a_keep, a_one, a_two, b_keep, b_one, b_two, out_ref):
    half = a_two.shape[0]
    for first, keep, one, two in ((0, a_keep, a_one, a_two), (half, b_keep, b_one, b_two)):
        for row in range(0, half, 128):
            rows = slice(row, row + 128)
            total = add(keep[0, rows], one[0, rows], two[rows])
            out_ref[:, first + row : first + row + 128] = total.T.astype(out_ref.dtype)


def sum_partials(flat):
    rows, samples = flat.shape[0], flat.shape[1] // (N_X * N_CORE)
    half = rows // 2
    h = lax.axis_index("hst")
    x, core = h // N_CORE, h % N_CORE
    column = (x ^ jnp.array([0, 3, 1, 2], jnp.int32)) * N_CORE
    params = pltpu.CompilerParams(vmem_limit_bytes=VMEM)
    block = pl.BlockSpec((rows, samples), lambda j, c: (j, 0))
    picked = pl.BlockSpec((rows, samples), lambda j, c: (0, c[j]))
    given = pl.pallas_call(
        pack_kernel,
        out_shape=jax.ShapeDtypeStruct((N_X * rows, samples), flat.dtype),
        grid_spec=pltpu.PrefetchScalarGridSpec(
            num_scalar_prefetch=1, grid=(N_X,), in_specs=[picked], out_specs=block
        ),
        compiler_params=params,
        name="pack",
    )(column + (1 - core), flat)
    got = lax.ppermute(given, "hst", CORE_SWAP)

    def half_block(index):
        return pl.BlockSpec((1, half, samples), lambda j, c: (index(j), 0, 0))

    a_keep, a_send, b_keep, b_send = pl.pallas_call(
        pair_kernel,
        out_shape=[jax.ShapeDtypeStruct((2, half, samples), flat.dtype)] * 4,
        grid_spec=pltpu.PrefetchScalarGridSpec(
            num_scalar_prefetch=1,
            grid=(N_X,),
            in_specs=[picked, block],
            out_specs=[
                half_block(lambda j: jnp.minimum(j, 1)),
                half_block(lambda j: j // 3),
                half_block(lambda j: j // 2),
                half_block(lambda j: j // 3),
            ],
        ),
        compiler_params=params,
        name="pair",
    )(column + core, flat, got)
    a_one = lax.ppermute(a_send, "hst", X_EVEN)
    b_one = lax.ppermute(b_send, "hst", X_ODD)
    a_two = lax.ppermute(add(a_keep[1], a_one[1]).astype(flat.dtype), "hst", X_ODD)
    b_two = lax.ppermute(add(b_keep[1], b_one[1]).astype(flat.dtype), "hst", X_EVEN)
    return pl.pallas_call(
        turn_kernel,
        out_shape=jax.ShapeDtypeStruct((samples, rows), flat.dtype),
        compiler_params=params,
        name="turn",
    )(a_keep, a_one, a_two, b_keep, b_one, b_two)


def normalize(flat_rows, ln_gain):
    middle = jnp.mean(flat_rows, axis=-1, keepdims=True)
    centered = flat_rows - middle
    variance = jnp.mean(centered * centered, axis=-1, keepdims=True)
    return (centered * lax.rsqrt(variance + 1e-05) * ln_gain).astype(jnp.bfloat16)


def gather_nodes(block):
    near = jnp.concatenate([block, lax.ppermute(block, "node", Z_NEAR)], 0)
    line = jnp.concatenate([near, lax.ppermute(near, "node", Z_FAR)], 0)
    half = line.shape[0] // 2
    even, odd = line, line
    blocks = [line]
    for _ in range(3):
        even, odd = lax.ppermute(odd, "node", Y_EVEN), lax.ppermute(even, "node", Y_ODD)
        blocks += [even, odd]
    blocks.append(lax.ppermute(odd[:half], "node", Y_EVEN))
    blocks.append(lax.ppermute(even[half:], "node", Y_ODD))
    return jnp.concatenate(blocks, 0)


def node_order():
    n = lax.axis_index("node")
    y, z = n // N_Z, n % N_Z
    sign = 1 - 2 * (y % 2)
    step = jnp.arange(N_Y * N_Z)
    nodes = (y + sign * jnp.array(Y_DISTANCE)[step // N_Z]) % N_Y * N_Z + (z ^ (step % N_Z))
    slots = jnp.array(Y_SLOT)[(sign * (step // N_Z - y)) % N_Y] * N_Z + (z ^ (step % N_Z))
    return nodes, slots


def local(partials, counts, perm, fm_proj, ln_gain, w_in, d_hidden):
    samples = counts.shape[2]
    group, hidden_here = d_hidden.shape[2], d_hidden.shape[3]
    w_full = lax.all_gather(w_in, "hst", axis=0, tiled=True)

    nodes, slots = node_order()
    d_hid = jnp.take(d_hidden[0, 0].reshape(-1, samples, hidden_here), nodes, axis=0, mode="clip")
    d_hid = d_hid.reshape(group, hidden_here)

    rows = partials.shape[2] * partials.shape[3]
    summed = sum_partials(partials[0].transpose(1, 2, 0).reshape(rows, -1))
    shard_rows = lax.all_to_all(
        summed.reshape(N_Y * N_Z, samples, rows), "node", split_axis=0, concat_axis=0, tiled=True
    )
    shard_rows = shard_rows.transpose(1, 0, 2).reshape(samples, -1, partials.shape[3])
    ordered = jnp.take(shard_rows, perm, axis=1, mode="clip")
    counts_here = counts[0, 0]
    divisor = jnp.maximum(counts_here, 1).astype(jnp.float32)[:, :, None]
    pooled = jnp.where(
        counts_here[:, :, None] > 0, ordered.astype(jnp.float32) / divisor, 0.0
    ).astype(jnp.bfloat16)
    projected = jnp.einsum(
        "sfe,fk->sek", pooled, fm_proj, preferred_element_type=jnp.float32
    ).astype(jnp.bfloat16)
    pairwise = jnp.einsum("sfe,sek->sfk", pooled, projected, preferred_element_type=jnp.float32)
    z_local = normalize(pairwise.reshape(samples, -1), ln_gain)

    z_group = gather_nodes(z_local)
    pre_act = jnp.dot(z_group, w_full, preferred_element_type=jnp.float32)
    sigma = jax.nn.sigmoid(pre_act)
    hidden = (pre_act * sigma).astype(jnp.bfloat16).reshape(-1, samples, hidden_here)
    hidden = jnp.take(hidden, slots, axis=0, mode="clip")
    d_pre = (d_hid.astype(jnp.float32) * sigma * (1.0 + pre_act * (1.0 - sigma))).astype(
        jnp.bfloat16
    )
    term = lax.dot_general(
        z_group, d_pre, (((0,), (0,)), ((), ())), preferred_element_type=jnp.float32
    ).astype(jnp.bfloat16)
    terms = lax.all_to_all(
        term.reshape(N_X * N_CORE, w_in.shape[0], hidden_here), "hst", 0, 0, tiled=True
    )
    share = add(*[terms[i] for i in range(N_X * N_CORE)]).astype(jnp.bfloat16)
    other = lax.ppermute(share, "dp", DP_SWAP)
    grad_w = add(share, other)
    return (hidden.reshape(1, 1, group, hidden_here), grad_w)


def solution(mesh):
    in_specs = (
        P("hst", "dp", "node", None),
        P("dp", "hst", "node", None),
        P(),
        P(),
        P(),
        P("hst", "node"),
        P("dp", "hst", None, "node"),
    )
    out_specs = (P("dp", "hst", None, "node"), P("hst", "node"))
    return jax.shard_map(local, mesh=mesh, in_specs=in_specs, out_specs=out_specs, check_vma=False)
```

```python
import jax
import jax.numpy as jnp
from jax import lax
from jax.experimental import pallas as pl
from jax.experimental.pallas import tpu as pltpu
from jax.sharding import PartitionSpec as P

N_X = 4
N_CORE = 2
N_Y = 8
N_Z = 4
VMEM = 12 * 2**20

def swaps(size, partner):
    return [(i, partner(i)) for i in range(size)]


CORE_SWAP = swaps(N_X * N_CORE, lambda h: h ^ 1)
X_EVEN = swaps(N_X * N_CORE, lambda h: h ^ 2)
X_ODD = swaps(N_X * N_CORE, lambda h: h ^ 6)
Z_NEAR = swaps(N_Y * N_Z, lambda n: n ^ 1)
Z_FAR = swaps(N_Y * N_Z, lambda n: n ^ 2)
DEVICES = N_Y * N_Z * N_X * N_CORE


def y_partner(device, odd):
    node, h = device // (N_X * N_CORE), device % (N_X * N_CORE)
    y = ((node // N_Z + odd) ^ 1) - odd
    return (y % N_Y * N_Z + node % N_Z) * N_X * N_CORE + h


Y_FIRST = swaps(DEVICES, lambda i: y_partner(i, i % N_CORE))
Y_SECOND = swaps(DEVICES, lambda i: y_partner(i, 1 - i % N_CORE))
DP_SWAP = swaps(2, lambda d: d ^ 1)
Y_DISTANCE = (0, 1, -1, 2, -2, 3, -3, 4)
Y_SLOT = (0, 1, 3, 5, 7, 6, 4, 2)
Z_STEP = (0, 2, 1, 3)


def add(*terms):
    total = terms[0].astype(jnp.float32)
    for term in terms[1:]:
        total = total + term.astype(jnp.float32)
    return total


def pack_kernel(h_ref, rows_ref, out_ref):
    out_ref[...] = rows_ref[...]


def pair_kernel(h_ref, rows_ref, got_ref, a_keep, a_send, b_keep, b_send):
    step = pl.program_id(0)
    total = add(rows_ref[...], got_ref[...]).astype(a_keep.dtype)
    half = total.shape[0] // 2

    @pl.when(step <= 1)
    def _():
        a_keep[0] = total[:half]

    @pl.when(step >= 2)
    def _():
        a_send[0] = total[:half]

    @pl.when((step == 0) | (step == 3))
    def _():
        b_keep[0] = total[half:]

    @pl.when((step == 1) | (step == 2))
    def _():
        b_send[0] = total[half:]


def turn_kernel(a_keep, a_one, a_two, b_keep, b_one, b_two, out_ref):
    half = a_two.shape[0]
    for first, keep, one, two in ((0, a_keep, a_one, a_two), (half, b_keep, b_one, b_two)):
        for row in range(0, half, 128):
            rows = slice(row, row + 128)
            total = add(keep[0, rows], one[0, rows], two[rows])
            out_ref[:, first + row : first + row + 128] = total.T.astype(out_ref.dtype)


def sum_partials(flat):
    rows, samples = flat.shape[0], flat.shape[1] // (N_X * N_CORE)
    half = rows // 2
    h = lax.axis_index("hst").astype(jnp.int32).reshape(1)
    params = pltpu.CompilerParams(vmem_limit_bytes=VMEM)
    block = pl.BlockSpec((rows, samples), lambda j, h: (j, 0))
    theirs = pl.BlockSpec((rows, samples), lambda j, h: (0, h[0] ^ 1 ^ (6 * j % 8)))
    mine = pl.BlockSpec((rows, samples), lambda j, h: (0, h[0] ^ (6 * j % 8)))
    given = pl.pallas_call(
        pack_kernel,
        out_shape=jax.ShapeDtypeStruct((N_X * rows, samples), flat.dtype),
        grid_spec=pltpu.PrefetchScalarGridSpec(
            num_scalar_prefetch=1, grid=(N_X,), in_specs=[theirs], out_specs=block
        ),
        compiler_params=params,
        name="pack",
    )(h, flat)
    got = lax.ppermute(given, "hst", CORE_SWAP)

    def half_block(index):
        return pl.BlockSpec((1, half, samples), lambda j, h: (index(j), 0, 0))

    a_keep, a_send, b_keep, b_send = pl.pallas_call(
        pair_kernel,
        out_shape=[jax.ShapeDtypeStruct((2, half, samples), flat.dtype)] * 4,
        grid_spec=pltpu.PrefetchScalarGridSpec(
            num_scalar_prefetch=1,
            grid=(N_X,),
            in_specs=[mine, block],
            out_specs=[
                half_block(lambda j: jnp.minimum(j, 1)),
                half_block(lambda j: 1 - j // 3),
                half_block(lambda j: j // 3),
                half_block(lambda j: j // 2),
            ],
        ),
        compiler_params=params,
        name="pair",
    )(h, flat, got)
    a_one = lax.ppermute(a_send, "hst", X_EVEN)
    b_one = lax.ppermute(b_send, "hst", X_ODD)
    a_two = lax.ppermute(add(a_keep[1], a_one[1]).astype(flat.dtype), "hst", X_ODD)
    b_two = lax.ppermute(add(b_keep[1], b_one[1]).astype(flat.dtype), "hst", X_EVEN)
    return pl.pallas_call(
        turn_kernel,
        out_shape=jax.ShapeDtypeStruct((samples, rows), flat.dtype),
        compiler_params=params,
        name="turn",
    )(a_keep, a_one, a_two, b_keep, b_one, b_two)


def normalize(flat_rows, ln_gain):
    middle = jnp.mean(flat_rows, axis=-1, keepdims=True)
    centered = flat_rows - middle
    variance = jnp.mean(centered * centered, axis=-1, keepdims=True)
    return (centered * lax.rsqrt(variance + 1e-05) * ln_gain).astype(jnp.bfloat16)


def gather_nodes(block):
    far = jnp.concatenate([block, lax.ppermute(block, "node", Z_FAR)], 0)
    line = jnp.concatenate([far, lax.ppermute(far, "node", Z_NEAR)], 0)
    half = line.shape[0] // 2

    def step(rows, pairs):
        return lax.ppermute(rows, ("node", "hst"), pairs)

    first, second = line, line
    blocks = [line]
    for _ in range(3):
        first, second = step(second, Y_FIRST), step(first, Y_SECOND)
        blocks += [first, second]
    blocks.append(step(second[:half], Y_FIRST))
    blocks.append(step(first[half:], Y_SECOND))
    return jnp.concatenate(blocks, 0)


def node_order():
    n = lax.axis_index("node")
    y, z = n // N_Z, n % N_Z
    sign = (1 - 2 * (y % 2)) * (1 - 2 * (lax.axis_index("hst") % N_CORE))
    step = jnp.arange(N_Y * N_Z)
    turn = jnp.array(Z_STEP)
    nodes = (y + sign * jnp.array(Y_DISTANCE)[step // N_Z]) % N_Y * N_Z + (z ^ turn[step % N_Z])
    slots = jnp.array(Y_SLOT)[sign * (step // N_Z - y) % N_Y] * N_Z + turn[z ^ (step % N_Z)]
    return nodes, slots


def local(partials, counts, perm, fm_proj, ln_gain, w_in, d_hidden):
    samples = counts.shape[2]
    group, hidden_here = d_hidden.shape[2], d_hidden.shape[3]
    nodes, slots = node_order()
    d_hid = jnp.take(d_hidden[0, 0].reshape(-1, samples, hidden_here), nodes, axis=0, mode="clip")
    d_hid = d_hid.reshape(group, hidden_here)

    rows = partials.shape[2] * partials.shape[3]
    summed = sum_partials(partials[0].transpose(1, 2, 0).reshape(rows, -1))
    summed, w_in = lax.optimization_barrier((summed, w_in))
    w_full = lax.all_gather(w_in, "hst", axis=0, tiled=True)
    shard_rows = lax.all_to_all(
        summed.reshape(N_Y * N_Z, samples, rows), "node", split_axis=0, concat_axis=0, tiled=True
    )
    shard_rows = shard_rows.transpose(1, 0, 2).reshape(samples, -1, partials.shape[3])
    ordered = jnp.take(shard_rows, perm, axis=1, mode="clip")
    counts_here = counts[0, 0]
    divisor = jnp.maximum(counts_here, 1).astype(jnp.float32)[:, :, None]
    pooled = jnp.where(
        counts_here[:, :, None] > 0, ordered.astype(jnp.float32) / divisor, 0.0
    ).astype(jnp.bfloat16)
    projected = jnp.einsum(
        "sfe,fk->sek", pooled, fm_proj, preferred_element_type=jnp.float32
    ).astype(jnp.bfloat16)
    pairwise = jnp.einsum("sfe,sek->sfk", pooled, projected, preferred_element_type=jnp.float32)
    z_local = normalize(pairwise.reshape(samples, -1), ln_gain)

    z_group = gather_nodes(z_local)
    pre_act = jnp.dot(z_group, w_full, preferred_element_type=jnp.float32)
    sigma = jax.nn.sigmoid(pre_act)
    hidden = (pre_act * sigma).astype(jnp.bfloat16).reshape(-1, samples, hidden_here)
    hidden = jnp.take(hidden, slots, axis=0, mode="clip")
    d_pre = (d_hid.astype(jnp.float32) * sigma * (1.0 + pre_act * (1.0 - sigma))).astype(
        jnp.bfloat16
    )
    term = lax.dot_general(
        z_group, d_pre, (((0,), (0,)), ((), ())), preferred_element_type=jnp.float32
    ).astype(jnp.bfloat16)
    term = term.reshape(N_X * N_CORE, w_in.shape[0], hidden_here)
    half = w_in.shape[0] // 2
    shares, others = [], []
    for rows in (slice(0, half), slice(half, None)):
        terms = lax.all_to_all(term[:, rows], "hst", 0, 0, tiled=True)
        shares.append(add(*[terms[i] for i in range(N_X * N_CORE)]).astype(jnp.bfloat16))
        others.append(lax.ppermute(shares[-1], "dp", DP_SWAP))
    grad_w = jnp.concatenate([add(*both) for both in zip(shares, others)], 0)
    return (hidden.reshape(1, 1, group, hidden_here), grad_w)


def solution(mesh):
    in_specs = (
        P("hst", "dp", "node", None),
        P("dp", "hst", "node", None),
        P(),
        P(),
        P(),
        P("hst", "node"),
        P("dp", "hst", None, "node"),
    )
    out_specs = (P("dp", "hst", None, "node"), P("hst", "node"))
    return jax.shard_map(local, mesh=mesh, in_specs=in_specs, out_specs=out_specs, check_vma=False)
```

```python
import jax
import jax.numpy as jnp
from jax import lax
from jax.experimental import pallas as pl
from jax.experimental.pallas import tpu as pltpu
from jax.sharding import PartitionSpec as P

N_X = 4
N_CORE = 2
N_Y = 8
N_Z = 4
VMEM = 12 * 2**20

def swaps(size, partner):
    return [(i, partner(i)) for i in range(size)]


CORE_SWAP = swaps(N_X * N_CORE, lambda h: h ^ 1)
X_EVEN = swaps(N_X * N_CORE, lambda h: h ^ 2)
X_ODD = swaps(N_X * N_CORE, lambda h: h ^ 6)
Y_EVEN = swaps(N_Y * N_Z, lambda n: n ^ N_Z)
Y_ODD = swaps(N_Y * N_Z, lambda n: (((n // N_Z + 1) ^ 1) - 1) % N_Y * N_Z + n % N_Z)
Y_GROUPS = [[N_Z * y + z for y in range(N_Y)] for z in range(N_Z)]
Z_GROUPS = [[N_Z * y + z for z in range(N_Z)] for y in range(N_Y)]
DP_SWAP = swaps(2, lambda d: d ^ 1)


def add(*terms):
    total = terms[0].astype(jnp.float32)
    for term in terms[1:]:
        total = total + term.astype(jnp.float32)
    return total


def pack_kernel(h_ref, rows_ref, out_ref):
    out_ref[...] = rows_ref[...]


def pair_kernel(h_ref, rows_ref, got_ref, a_keep, a_send, b_keep, b_send):
    step = pl.program_id(0)
    total = add(rows_ref[...], got_ref[...]).astype(a_keep.dtype)
    half = total.shape[0] // 2

    @pl.when(step <= 1)
    def _():
        a_keep[0] = total[:half]

    @pl.when(step >= 2)
    def _():
        a_send[0] = total[:half]

    @pl.when((step == 0) | (step == 3))
    def _():
        b_keep[0] = total[half:]

    @pl.when((step == 1) | (step == 2))
    def _():
        b_send[0] = total[half:]


def turn_kernel(a_keep, a_one, a_two, b_keep, b_one, b_two, out_ref):
    half = a_two.shape[0]
    for first, keep, one, two in ((0, a_keep, a_one, a_two), (half, b_keep, b_one, b_two)):
        for row in range(0, half, 128):
            rows = slice(row, row + 128)
            total = add(keep[0, rows], one[0, rows], two[rows])
            out_ref[:, first + row : first + row + 128] = total.T.astype(out_ref.dtype)


def sum_partials(flat):
    rows, samples = flat.shape[0], flat.shape[1] // (N_X * N_CORE)
    half = rows // 2
    h = lax.axis_index("hst").astype(jnp.int32).reshape(1)
    params = pltpu.CompilerParams(vmem_limit_bytes=VMEM)
    block = pl.BlockSpec((rows, samples), lambda j, h: (j, 0))
    theirs = pl.BlockSpec((rows, samples), lambda j, h: (0, h[0] ^ 1 ^ (6 * j % 8)))
    mine = pl.BlockSpec((rows, samples), lambda j, h: (0, h[0] ^ (6 * j % 8)))
    given = pl.pallas_call(
        pack_kernel,
        out_shape=jax.ShapeDtypeStruct((N_X * rows, samples), flat.dtype),
        grid_spec=pltpu.PrefetchScalarGridSpec(
            num_scalar_prefetch=1, grid=(N_X,), in_specs=[theirs], out_specs=block
        ),
        compiler_params=pltpu.CompilerParams(vmem_limit_bytes=4 * VMEM),
        name="pack",
    )(h, flat)
    got = lax.ppermute(given, "hst", CORE_SWAP)

    def half_block(index):
        return pl.BlockSpec((1, half, samples), lambda j, h: (index(j), 0, 0))

    a_keep, a_send, b_keep, b_send = pl.pallas_call(
        pair_kernel,
        out_shape=[jax.ShapeDtypeStruct((2, half, samples), flat.dtype)] * 4,
        grid_spec=pltpu.PrefetchScalarGridSpec(
            num_scalar_prefetch=1,
            grid=(N_X,),
            in_specs=[mine, block],
            out_specs=[
                half_block(lambda j: jnp.minimum(j, 1)),
                half_block(lambda j: 1 - j // 3),
                half_block(lambda j: j // 3),
                half_block(lambda j: j // 2),
            ],
        ),
        compiler_params=params,
        name="pair",
    )(h, flat, got)
    a_one = lax.ppermute(a_send, "hst", X_EVEN)
    b_one = lax.ppermute(b_send, "hst", X_ODD)
    a_two = lax.ppermute(add(a_keep[1], a_one[1]).astype(flat.dtype), "hst", X_ODD)
    b_two = lax.ppermute(add(b_keep[1], b_one[1]).astype(flat.dtype), "hst", X_EVEN)
    return pl.pallas_call(
        turn_kernel,
        out_shape=jax.ShapeDtypeStruct((samples, rows), flat.dtype),
        compiler_params=params,
        name="turn",
    )(a_keep, a_one, a_two, b_keep, b_one, b_two)


def normalize(flat_rows, ln_gain):
    middle = jnp.mean(flat_rows, axis=-1, keepdims=True)
    centered = flat_rows - middle
    variance = jnp.mean(centered * centered, axis=-1, keepdims=True)
    return (centered * lax.rsqrt(variance + 1e-05) * ln_gain).astype(jnp.bfloat16)


def gather_nodes(block):
    copies = jnp.broadcast_to(block, (N_Z,) + block.shape)
    line = lax.all_to_all(copies, "node", 0, 0, axis_index_groups=Z_GROUPS, tiled=True)
    line = line.reshape(-1, block.shape[1])
    rows, width = line.shape[0], line.shape[1] // 2
    right = lax.all_gather(
        line[:, width:], "node", axis_index_groups=Y_GROUPS, axis=0, tiled=True
    )
    y = lax.axis_index("node") // N_Z
    sign = 1 - 2 * (y % 2)

    def put(left, part, distance, first_row=0):
        place = (y + sign * distance) % N_Y * rows + first_row
        return lax.dynamic_update_slice(left, part, (place, 0))

    even = odd = line[:, :width]
    left = put(jnp.zeros((N_Y * rows, width), line.dtype), even, 0)
    for distance in range(1, N_Y // 2):
        even, odd = lax.ppermute(odd, "node", Y_EVEN), lax.ppermute(even, "node", Y_ODD)
        left = put(put(left, even, distance), odd, -distance)
    half = rows // 2
    even = lax.ppermute(odd[:half], "node", Y_EVEN), lax.ppermute(even[half:], "node", Y_ODD)
    left = put(put(left, even[0], N_Y // 2), even[1], N_Y // 2, half)
    return left, right


def local(partials, counts, perm, fm_proj, ln_gain, w_in, d_hidden):
    samples = counts.shape[2]
    group, hidden_here = d_hidden.shape[2], d_hidden.shape[3]
    w_full = lax.all_gather(w_in, "hst", axis=0, tiled=True)
    rows = partials.shape[2] * partials.shape[3]
    summed = sum_partials(partials[0].transpose(1, 2, 0).reshape(rows, -1))
    shard_rows = lax.all_to_all(
        summed.reshape(N_Y * N_Z, samples, rows), "node", split_axis=0, concat_axis=0, tiled=True
    )
    shard_rows = shard_rows.transpose(1, 0, 2).reshape(samples, -1, partials.shape[3])
    ordered = jnp.take(shard_rows, perm, axis=1, mode="clip")
    counts_here = counts[0, 0]
    divisor = jnp.maximum(counts_here, 1).astype(jnp.float32)[:, :, None]
    pooled = jnp.where(
        counts_here[:, :, None] > 0, ordered.astype(jnp.float32) / divisor, 0.0
    ).astype(jnp.bfloat16)
    projected = jnp.einsum(
        "sfe,fk->sek", pooled, fm_proj, preferred_element_type=jnp.float32
    ).astype(jnp.bfloat16)
    pairwise = jnp.einsum("sfe,sek->sfk", pooled, projected, preferred_element_type=jnp.float32)
    z_local = normalize(pairwise.reshape(samples, -1), ln_gain)

    left, right = gather_nodes(z_local)
    width = left.shape[1]
    pre_act = jnp.dot(left, w_full[:width], preferred_element_type=jnp.float32)
    pre_act = pre_act + jnp.dot(right, w_full[width:], preferred_element_type=jnp.float32)
    sigma = jax.nn.sigmoid(pre_act)
    hidden = (pre_act * sigma).astype(jnp.bfloat16)
    d_pre = (d_hidden[0, 0].astype(jnp.float32) * sigma * (1.0 + pre_act * (1.0 - sigma))).astype(
        jnp.bfloat16
    )
    term = [
        lax.dot_general(
            part, d_pre, (((0,), (0,)), ((), ())), preferred_element_type=jnp.float32
        ).astype(jnp.bfloat16)
        for part in (left, right)
    ]
    term = jnp.concatenate(term, 0).reshape(N_X * N_CORE, w_in.shape[0], hidden_here)
    terms = lax.all_to_all(term, "hst", 0, 0, tiled=True)
    share = add(*[terms[i] for i in range(N_X * N_CORE)]).astype(jnp.bfloat16)
    grad_w = add(share, lax.ppermute(share, "dp", DP_SWAP))
    return (hidden.reshape(1, 1, group, hidden_here), grad_w)


def solution(mesh):
    in_specs = (
        P("hst", "dp", "node", None),
        P("dp", "hst", "node", None),
        P(),
        P(),
        P(),
        P("hst", "node"),
        P("dp", "hst", None, "node"),
    )
    out_specs = (P("dp", "hst", None, "node"), P("hst", "node"))
    return jax.shard_map(local, mesh=mesh, in_specs=in_specs, out_specs=out_specs, check_vma=False)
```

```python
import jax
import jax.numpy as jnp
from jax import lax
from jax.experimental import pallas as pl
from jax.experimental.pallas import tpu as pltpu
from jax.sharding import PartitionSpec as P

N_X = 4
N_CORE = 2
N_Y = 8
N_Z = 4
VMEM = 12 * 2**20

def swaps(size, partner):
    return [(i, partner(i)) for i in range(size)]


CORE_SWAP = swaps(N_X * N_CORE, lambda h: h ^ 1)
X_EVEN = swaps(N_X * N_CORE, lambda h: h ^ 2)
X_ODD = swaps(N_X * N_CORE, lambda h: h ^ 6)
Y_EVEN = swaps(N_Y * N_Z, lambda n: n ^ N_Z)
Y_ODD = swaps(N_Y * N_Z, lambda n: (((n // N_Z + 1) ^ 1) - 1) % N_Y * N_Z + n % N_Z)
Z_GROUPS = [[N_Z * y + z for z in range(N_Z)] for y in range(N_Y)]
X_GROUPS = [[N_CORE * x + c for x in range(N_X)] for c in range(N_CORE)]
DP_SWAP = swaps(2, lambda d: d ^ 1)


def add(*terms):
    total = terms[0].astype(jnp.float32)
    for term in terms[1:]:
        total = total + term.astype(jnp.float32)
    return total


def pack_kernel(h_ref, rows_ref, out_ref):
    out_ref[...] = rows_ref[...]


def pair_kernel(h_ref, rows_ref, got_ref, *out_refs):
    total = add(rows_ref[...], got_ref[...]).astype(rows_ref.dtype)
    half = total.shape[0] // 2
    for j in range(N_X):

        @pl.when(pl.program_id(0) == j)
        def _(away=-j % N_X):
            out_refs[away][...] = total[:half]
            out_refs[N_X + away][...] = total[half:]


def turn_kernel(*refs):
    out_ref = refs[-1]
    half = refs[0].shape[0]
    for first, parts in ((0, refs[:3]), (half, refs[3:6])):
        for row in range(0, half, 128):
            total = add(*[part[row : row + 128] for part in parts])
            out_ref[:, first + row : first + row + 128] = total.T.astype(out_ref.dtype)


def sum_partials(flat):
    rows, samples = flat.shape[0], flat.shape[1] // (N_X * N_CORE)
    half = rows // 2
    h = lax.axis_index("hst").astype(jnp.int32).reshape(1)
    params = pltpu.CompilerParams(vmem_limit_bytes=VMEM)
    block = pl.BlockSpec((rows, samples), lambda j, h: (j, 0))
    theirs = pl.BlockSpec((rows, samples), lambda j, h: (0, h[0] ^ 1 ^ (6 * j % 8)))
    mine = pl.BlockSpec((rows, samples), lambda j, h: (0, h[0] ^ (6 * j % 8)))
    given = pl.pallas_call(
        pack_kernel,
        out_shape=jax.ShapeDtypeStruct((N_X * rows, samples), flat.dtype),
        grid_spec=pltpu.PrefetchScalarGridSpec(
            num_scalar_prefetch=1, grid=(N_X,), in_specs=[theirs], out_specs=block
        ),
        compiler_params=pltpu.CompilerParams(vmem_limit_bytes=4 * VMEM),
        name="pack",
    )(h, flat)
    got = lax.ppermute(given, "hst", CORE_SWAP)

    out = pl.pallas_call(
        pair_kernel,
        out_shape=[jax.ShapeDtypeStruct((half, samples), flat.dtype)] * (2 * N_X),
        grid_spec=pltpu.PrefetchScalarGridSpec(
            num_scalar_prefetch=1,
            grid=(N_X,),
            in_specs=[mine, block],
            out_specs=[pl.BlockSpec((half, samples), lambda j, h: (0, 0))] * (2 * N_X),
        ),
        compiler_params=params,
        name="pair",
    )(h, flat, got)
    a, b = out[:N_X], out[N_X:]
    a_far = lax.ppermute(a[2], "hst", X_EVEN)
    b_far = lax.ppermute(b[2], "hst", X_ODD)
    a_one = lax.ppermute(a[1], "hst", X_EVEN)
    b_one = lax.ppermute(b[3], "hst", X_ODD)
    a_two = lax.ppermute(add(a[3], a_far).astype(flat.dtype), "hst", X_ODD)
    b_two = lax.ppermute(add(b[1], b_far).astype(flat.dtype), "hst", X_EVEN)
    return pl.pallas_call(
        turn_kernel,
        out_shape=jax.ShapeDtypeStruct((samples, rows), flat.dtype),
        compiler_params=params,
        name="turn",
    )(a[0], a_one, a_two, b[0], b_one, b_two)


def normalize(flat_rows, ln_gain):
    middle = jnp.mean(flat_rows, axis=-1, keepdims=True)
    centered = flat_rows - middle
    variance = jnp.mean(centered * centered, axis=-1, keepdims=True)
    return (centered * lax.rsqrt(variance + 1e-05) * ln_gain).astype(jnp.bfloat16)


def gather_nodes(block):
    copies = jnp.broadcast_to(block, (N_Z,) + block.shape)
    line = lax.all_to_all(copies, "node", 0, 0, axis_index_groups=Z_GROUPS, tiled=True)
    line = line.reshape(-1, block.shape[1])
    rows, half = line.shape[0], line.shape[0] // 2
    y = lax.axis_index("node") // N_Z
    sign = 1 - 2 * (y % 2)

    def put(group, part, distance, first_row=0):
        place = (y + sign * distance) % N_Y * rows + first_row
        return lax.dynamic_update_slice(group, part, (place, 0))

    even = odd = line
    group = put(jnp.zeros((N_Y * rows, line.shape[1]), line.dtype), line, 0)
    for distance in range(1, N_Y // 2):
        even, odd = lax.ppermute(odd, "node", Y_EVEN), lax.ppermute(even, "node", Y_ODD)
        group = put(put(group, even, distance), odd, -distance)
    even, odd = lax.ppermute(odd[:half], "node", Y_EVEN), lax.ppermute(even[half:], "node", Y_ODD)
    return put(put(group, even, N_Y // 2), odd, N_Y // 2, half)


def local(partials, counts, perm, fm_proj, ln_gain, w_in, d_hidden):
    samples = counts.shape[2]
    group, hidden_here = d_hidden.shape[2], d_hidden.shape[3]
    w_full = lax.all_gather(w_in, "hst", axis=0, tiled=True)
    rows = partials.shape[2] * partials.shape[3]
    summed = sum_partials(partials[0].transpose(1, 2, 0).reshape(rows, -1))
    shard_rows = lax.all_to_all(
        summed.reshape(N_Y * N_Z, samples, rows), "node", split_axis=0, concat_axis=0, tiled=True
    )
    shard_rows = shard_rows.transpose(1, 0, 2).reshape(samples, -1, partials.shape[3])
    ordered = jnp.take(shard_rows, perm, axis=1, mode="clip")
    counts_here = counts[0, 0]
    divisor = jnp.maximum(counts_here, 1).astype(jnp.float32)[:, :, None]
    pooled = jnp.where(
        counts_here[:, :, None] > 0, ordered.astype(jnp.float32) / divisor, 0.0
    ).astype(jnp.bfloat16)
    projected = jnp.einsum(
        "sfe,fk->sek", pooled, fm_proj, preferred_element_type=jnp.float32
    ).astype(jnp.bfloat16)
    pairwise = jnp.einsum("sfe,sek->sfk", pooled, projected, preferred_element_type=jnp.float32)
    z_local = normalize(pairwise.reshape(samples, -1), ln_gain)

    z_group = gather_nodes(z_local)
    pre_act = jnp.dot(z_group, w_full, preferred_element_type=jnp.float32)
    sigma = jax.nn.sigmoid(pre_act)
    hidden = (pre_act * sigma).astype(jnp.bfloat16)
    d_pre = (d_hidden[0, 0].astype(jnp.float32) * sigma * (1.0 + pre_act * (1.0 - sigma))).astype(
        jnp.bfloat16
    )
    term = lax.dot_general(
        z_group, d_pre, (((0,), (0,)), ((), ())), preferred_element_type=jnp.float32
    ).astype(jnp.bfloat16)
    term = term.reshape(N_X, N_CORE, w_in.shape[0], hidden_here)
    core = lax.axis_index("hst") % N_CORE
    given = lax.dynamic_index_in_dim(term, 1 - core, 1, keepdims=False)
    kept = lax.dynamic_index_in_dim(term, core, 1, keepdims=False)
    pair = add(kept, lax.ppermute(given, "hst", CORE_SWAP)).astype(jnp.bfloat16)
    terms = lax.all_to_all(pair, "hst", 0, 0, axis_index_groups=X_GROUPS, tiled=True)
    share = add(*[terms[i] for i in range(N_X)]).astype(jnp.bfloat16)
    grad_w = add(share, lax.ppermute(share, "dp", DP_SWAP))
    return (hidden.reshape(1, 1, group, hidden_here), grad_w)


def solution(mesh):
    in_specs = (
        P("hst", "dp", "node", None),
        P("dp", "hst", "node", None),
        P(),
        P(),
        P(),
        P("hst", "node"),
        P("dp", "hst", None, "node"),
    )
    out_specs = (P("dp", "hst", None, "node"), P("hst", "node"))
    return jax.shard_map(local, mesh=mesh, in_specs=in_specs, out_specs=out_specs, check_vma=False)
```

```python
import jax
import jax.numpy as jnp
from jax import lax
from jax.experimental import pallas as pl
from jax.experimental.pallas import tpu as pltpu
from jax.sharding import PartitionSpec as P

N_X = 4
N_CORE = 2
N_Y = 8
N_Z = 4
VMEM = 12 * 2**20

def swaps(size, partner):
    return [(i, partner(i)) for i in range(size)]


CORE_SWAP = swaps(N_X * N_CORE, lambda h: h ^ 1)
X_EVEN = swaps(N_X * N_CORE, lambda h: h ^ 2)
X_ODD = swaps(N_X * N_CORE, lambda h: h ^ 6)
DEVICES = N_Y * N_Z * N_X * N_CORE


def y_partner(device, odd):
    node, h = device // (N_X * N_CORE), device % (N_X * N_CORE)
    y = ((node // N_Z + odd) ^ 1) - odd
    return (y % N_Y * N_Z + node % N_Z) * N_X * N_CORE + h


Y_FIRST = swaps(DEVICES, lambda i: y_partner(i, i % N_CORE))
Y_SECOND = swaps(DEVICES, lambda i: y_partner(i, 1 - i % N_CORE))
Z_GROUPS = [[N_Z * y + z for z in range(N_Z)] for y in range(N_Y)]
X_GROUPS = [[N_CORE * x + c for x in range(N_X)] for c in range(N_CORE)]
DP_SWAP = swaps(2, lambda d: d ^ 1)


def add(*terms):
    total = terms[0].astype(jnp.float32)
    for term in terms[1:]:
        total = total + term.astype(jnp.float32)
    return total


def pack_kernel(h_ref, rows_ref, out_ref):
    out_ref[...] = rows_ref[...]


def pair_kernel(h_ref, rows_ref, got_ref, *out_refs):
    total = add(rows_ref[...], got_ref[...]).astype(rows_ref.dtype)
    half = total.shape[0] // 2
    for j in range(N_X):

        @pl.when(pl.program_id(0) == j)
        def _(away=-j % N_X):
            out_refs[away][...] = total[:half]
            out_refs[N_X + away][...] = total[half:]


def turn_kernel(*refs):
    out_ref = refs[-1]
    half = refs[0].shape[0]
    for first, parts in ((0, refs[:3]), (half, refs[3:6])):
        for row in range(0, half, 128):
            total = add(*[part[row : row + 128] for part in parts])
            out_ref[:, first + row : first + row + 128] = total.T.astype(out_ref.dtype)


def sum_partials(flat):
    rows, samples = flat.shape[0], flat.shape[1] // (N_X * N_CORE)
    half = rows // 2
    h = lax.axis_index("hst").astype(jnp.int32).reshape(1)
    params = pltpu.CompilerParams(vmem_limit_bytes=VMEM)
    block = pl.BlockSpec((rows, samples), lambda j, h: (j, 0))
    theirs = pl.BlockSpec((rows, samples), lambda j, h: (0, h[0] ^ 1 ^ (6 * j % 8)))
    mine = pl.BlockSpec((rows, samples), lambda j, h: (0, h[0] ^ (6 * j % 8)))
    given = pl.pallas_call(
        pack_kernel,
        out_shape=jax.ShapeDtypeStruct((N_X * rows, samples), flat.dtype),
        grid_spec=pltpu.PrefetchScalarGridSpec(
            num_scalar_prefetch=1, grid=(N_X,), in_specs=[theirs], out_specs=block
        ),
        compiler_params=pltpu.CompilerParams(vmem_limit_bytes=4 * VMEM),
        name="pack",
    )(h, flat)
    got = lax.ppermute(given, "hst", CORE_SWAP)

    out = pl.pallas_call(
        pair_kernel,
        out_shape=[jax.ShapeDtypeStruct((half, samples), flat.dtype)] * (2 * N_X),
        grid_spec=pltpu.PrefetchScalarGridSpec(
            num_scalar_prefetch=1,
            grid=(N_X,),
            in_specs=[mine, block],
            out_specs=[pl.BlockSpec((half, samples), lambda j, h: (0, 0))] * (2 * N_X),
        ),
        compiler_params=params,
        name="pair",
    )(h, flat, got)
    a, b = out[:N_X], out[N_X:]
    a_far = lax.ppermute(a[2], "hst", X_EVEN)
    b_far = lax.ppermute(b[2], "hst", X_ODD)
    a_one = lax.ppermute(a[1], "hst", X_EVEN)
    b_one = lax.ppermute(b[3], "hst", X_ODD)
    a_two = lax.ppermute(add(a[3], a_far).astype(flat.dtype), "hst", X_ODD)
    b_two = lax.ppermute(add(b[1], b_far).astype(flat.dtype), "hst", X_EVEN)
    return pl.pallas_call(
        turn_kernel,
        out_shape=jax.ShapeDtypeStruct((samples, rows), flat.dtype),
        compiler_params=params,
        name="turn",
    )(a[0], a_one, a_two, b[0], b_one, b_two)


def normalize(flat_rows, ln_gain):
    middle = jnp.mean(flat_rows, axis=-1, keepdims=True)
    centered = flat_rows - middle
    variance = jnp.mean(centered * centered, axis=-1, keepdims=True)
    return (centered * lax.rsqrt(variance + 1e-05) * ln_gain).astype(jnp.bfloat16)


def gather_nodes(block, early):
    copies = jnp.broadcast_to(block, (N_Z,) + block.shape)
    line = lax.all_to_all(copies, "node", 0, 0, axis_index_groups=Z_GROUPS, tiled=True)
    line = line.reshape(-1, block.shape[1])
    rows = line.shape[0]
    y, core = lax.axis_index("node") // N_Z, lax.axis_index("hst") % N_CORE
    sign = (1 - 2 * (y % 2)) * (1 - 2 * core)

    def put(group, part, distance):
        return lax.dynamic_update_slice(group, part, ((y + sign * distance) % N_Y * rows, 0))

    group = put(jnp.zeros((N_Y * rows, line.shape[1]), line.dtype), line, 0)
    both = jnp.concatenate([line, lax.ppermute(line, "hst", CORE_SWAP)], 0)
    handed = []
    for step in range(1, N_Y // 2):
        both = lax.ppermute(both, ("node", "hst"), Y_FIRST if step % 2 else Y_SECOND)
        group = put(group, both[:rows], step if step % 2 else -step)
        handed.append(both[rows:])
        if step == 1:
            both, early = lax.optimization_barrier((both, early))
    last = lax.ppermute(both[:rows], ("node", "hst"), Y_SECOND)
    handed = lax.ppermute(jnp.concatenate(handed, 0), "hst", CORE_SWAP)
    for step in range(1, N_Y // 2):
        part = handed[(step - 1) * rows : step * rows]
        group = put(group, part, -step if step % 2 else step)
    return put(group, last, N_Y // 2), early


def local(partials, counts, perm, fm_proj, ln_gain, w_in, d_hidden):
    samples = counts.shape[2]
    group, hidden_here = d_hidden.shape[2], d_hidden.shape[3]
    w_full = lax.all_gather(w_in, "hst", axis=0, tiled=True)
    rows = partials.shape[2] * partials.shape[3]
    summed = sum_partials(partials[0].transpose(1, 2, 0).reshape(rows, -1))
    shard_rows = lax.all_to_all(
        summed.reshape(N_Y * N_Z, samples, rows), "node", split_axis=0, concat_axis=0, tiled=True
    )
    shard_rows = shard_rows.transpose(1, 0, 2).reshape(samples, -1, partials.shape[3])
    ordered = jnp.take(shard_rows, perm, axis=1, mode="clip")
    counts_here = counts[0, 0]
    divisor = jnp.maximum(counts_here, 1).astype(jnp.float32)[:, :, None]
    pooled = jnp.where(
        counts_here[:, :, None] > 0, ordered.astype(jnp.float32) / divisor, 0.0
    ).astype(jnp.bfloat16)
    projected = jnp.einsum(
        "sfe,fk->sek", pooled, fm_proj, preferred_element_type=jnp.float32
    ).astype(jnp.bfloat16)
    pairwise = jnp.einsum("sfe,sek->sfk", pooled, projected, preferred_element_type=jnp.float32)
    z_local = normalize(pairwise.reshape(samples, -1), ln_gain)

    z_group, w_full = gather_nodes(z_local, w_full)
    pre_act = jnp.dot(z_group, w_full, preferred_element_type=jnp.float32)
    sigma = jax.nn.sigmoid(pre_act)
    hidden = (pre_act * sigma).astype(jnp.bfloat16)
    d_pre = (d_hidden[0, 0].astype(jnp.float32) * sigma * (1.0 + pre_act * (1.0 - sigma))).astype(
        jnp.bfloat16
    )
    term = lax.dot_general(
        z_group, d_pre, (((0,), (0,)), ((), ())), preferred_element_type=jnp.float32
    ).astype(jnp.bfloat16)
    term = term.reshape(N_X, N_CORE, w_in.shape[0], hidden_here)
    core = lax.axis_index("hst") % N_CORE
    given = lax.dynamic_index_in_dim(term, 1 - core, 1, keepdims=False)
    kept = lax.dynamic_index_in_dim(term, core, 1, keepdims=False)
    pair = add(kept, lax.ppermute(given, "hst", CORE_SWAP)).astype(jnp.bfloat16)
    terms = lax.all_to_all(pair, "hst", 0, 0, axis_index_groups=X_GROUPS, tiled=True)
    share = add(*[terms[i] for i in range(N_X)]).astype(jnp.bfloat16)
    grad_w = add(share, lax.ppermute(share, "dp", DP_SWAP))
    return (hidden.reshape(1, 1, group, hidden_here), grad_w)


def solution(mesh):
    in_specs = (
        P("hst", "dp", "node", None),
        P("dp", "hst", "node", None),
        P(),
        P(),
        P(),
        P("hst", "node"),
        P("dp", "hst", None, "node"),
    )
    out_specs = (P("dp", "hst", None, "node"), P("hst", "node"))
    return jax.shard_map(local, mesh=mesh, in_specs=in_specs, out_specs=out_specs, check_vma=False)
```

```python
import jax
import jax.numpy as jnp
from jax import lax
from jax.experimental import pallas as pl
from jax.experimental.pallas import tpu as pltpu
from jax.sharding import PartitionSpec as P

N_X = 4
N_CORE = 2
N_Y = 8
N_Z = 4
VMEM = 12 * 2**20

def swaps(size, partner):
    return [(i, partner(i)) for i in range(size)]


CORE_SWAP = swaps(N_X * N_CORE, lambda h: h ^ 1)
X_EVEN = swaps(N_X * N_CORE, lambda h: h ^ 2)
X_ODD = swaps(N_X * N_CORE, lambda h: h ^ 6)
Y_EVEN = swaps(N_Y * N_Z, lambda n: n ^ N_Z)
Y_ODD = swaps(N_Y * N_Z, lambda n: (((n // N_Z + 1) ^ 1) - 1) % N_Y * N_Z + n % N_Z)
Z_GROUPS = [[N_Z * y + z for z in range(N_Z)] for y in range(N_Y)]
X_GROUPS = [[N_CORE * x + c for x in range(N_X)] for c in range(N_CORE)]
DP_SWAP = swaps(2, lambda d: d ^ 1)


def add(*terms):
    total = terms[0].astype(jnp.float32)
    for term in terms[1:]:
        total = total + term.astype(jnp.float32)
    return total


def pack_kernel(h_ref, rows_ref, out_ref):
    out_ref[...] = rows_ref[...]


def pair_kernel(h_ref, rows_ref, got_ref, *out_refs):
    total = add(rows_ref[...], got_ref[...]).astype(rows_ref.dtype)
    half = total.shape[0] // 2
    for j in range(N_X):

        @pl.when(pl.program_id(0) == j)
        def _(away=-j % N_X):
            out_refs[away][...] = total[:half]
            out_refs[N_X + away][...] = total[half:]


def turn_kernel(*refs):
    out_ref = refs[-1]
    half = refs[0].shape[0]
    for first, parts in ((0, refs[:3]), (half, refs[3:6])):
        for row in range(0, half, 128):
            total = add(*[part[row : row + 128] for part in parts])
            out_ref[:, first + row : first + row + 128] = total.T.astype(out_ref.dtype)


def sum_partials(flat):
    rows, samples = flat.shape[0], flat.shape[1] // (N_X * N_CORE)
    half = rows // 2
    h = lax.axis_index("hst").astype(jnp.int32).reshape(1)
    params = pltpu.CompilerParams(vmem_limit_bytes=VMEM)
    block = pl.BlockSpec((rows, samples), lambda j, h: (j, 0))
    theirs = pl.BlockSpec((rows, samples), lambda j, h: (0, h[0] ^ 1 ^ (6 * j % 8)))
    mine = pl.BlockSpec((rows, samples), lambda j, h: (0, h[0] ^ (6 * j % 8)))
    given = pl.pallas_call(
        pack_kernel,
        out_shape=jax.ShapeDtypeStruct((N_X * rows, samples), flat.dtype),
        grid_spec=pltpu.PrefetchScalarGridSpec(
            num_scalar_prefetch=1, grid=(N_X,), in_specs=[theirs], out_specs=block
        ),
        compiler_params=pltpu.CompilerParams(vmem_limit_bytes=4 * VMEM),
        name="pack",
    )(h, flat)
    got = lax.ppermute(given, "hst", CORE_SWAP)

    out = pl.pallas_call(
        pair_kernel,
        out_shape=[jax.ShapeDtypeStruct((half, samples), flat.dtype)] * (2 * N_X),
        grid_spec=pltpu.PrefetchScalarGridSpec(
            num_scalar_prefetch=1,
            grid=(N_X,),
            in_specs=[mine, block],
            out_specs=[pl.BlockSpec((half, samples), lambda j, h: (0, 0))] * (2 * N_X),
        ),
        compiler_params=params,
        name="pair",
    )(h, flat, got)
    a, b = out[:N_X], out[N_X:]
    a_far = lax.ppermute(a[2], "hst", X_EVEN)
    b_far = lax.ppermute(b[2], "hst", X_ODD)
    a_one = lax.ppermute(a[1], "hst", X_EVEN)
    b_one = lax.ppermute(b[3], "hst", X_ODD)
    a_two = lax.ppermute(add(a[3], a_far).astype(flat.dtype), "hst", X_ODD)
    b_two = lax.ppermute(add(b[1], b_far).astype(flat.dtype), "hst", X_EVEN)
    return pl.pallas_call(
        turn_kernel,
        out_shape=jax.ShapeDtypeStruct((samples, rows), flat.dtype),
        compiler_params=params,
        name="turn",
    )(a[0], a_one, a_two, b[0], b_one, b_two)


def normalize(flat_rows, ln_gain):
    middle = jnp.mean(flat_rows, axis=-1, keepdims=True)
    centered = flat_rows - middle
    variance = jnp.mean(centered * centered, axis=-1, keepdims=True)
    return (centered * lax.rsqrt(variance + 1e-05) * ln_gain).astype(jnp.bfloat16)


def gather_nodes(block):
    copies = jnp.broadcast_to(block, (N_Z,) + block.shape)
    line = lax.all_to_all(copies, "node", 0, 0, axis_index_groups=Z_GROUPS, tiled=True)
    line = line.reshape(-1, block.shape[1])
    rows, half = line.shape[0], line.shape[0] // 2
    y = lax.axis_index("node") // N_Z
    sign = 1 - 2 * (y % 2)

    def put(group, part, distance, first_row=0):
        place = (y + sign * distance) % N_Y * rows + first_row
        return lax.dynamic_update_slice(group, part, (place, 0))

    group = put(jnp.zeros((N_Y * rows, line.shape[1]), line.dtype), line, 0)
    pairs = (Y_EVEN, Y_ODD)
    lead = lax.ppermute(line, "node", pairs[0])
    trail = lax.ppermute(line, "node", pairs[1])
    for step in range(1, N_Y // 2):
        pairs = pairs[::-1]
        way = step if step % 2 else -step
        group = put(put(group, lead, way), trail, -way)
        if step == N_Y // 2 - 1:
            lead, trail = lead[half:], trail[:half]
        lead, trail = lax.ppermute(lead, "node", pairs[0]), lax.ppermute(trail, "node", pairs[1])
    return put(put(group, lead, N_Y // 2, half), trail, N_Y // 2)


def local(partials, counts, perm, fm_proj, ln_gain, w_in, d_hidden):
    samples = counts.shape[2]
    group, hidden_here = d_hidden.shape[2], d_hidden.shape[3]
    w_full = lax.all_gather(w_in, "hst", axis=0, tiled=True)
    rows = partials.shape[2] * partials.shape[3]
    summed = sum_partials(partials[0].transpose(1, 2, 0).reshape(rows, -1))
    shard_rows = lax.all_to_all(
        summed.reshape(N_Y * N_Z, samples, rows), "node", split_axis=0, concat_axis=0, tiled=True
    )
    shard_rows = shard_rows.transpose(1, 0, 2).reshape(samples, -1, partials.shape[3])
    ordered = jnp.take(shard_rows, perm, axis=1, mode="clip")
    counts_here = counts[0, 0]
    divisor = jnp.maximum(counts_here, 1).astype(jnp.float32)[:, :, None]
    pooled = jnp.where(
        counts_here[:, :, None] > 0, ordered.astype(jnp.float32) / divisor, 0.0
    ).astype(jnp.bfloat16)
    projected = jnp.einsum(
        "sfe,fk->sek", pooled, fm_proj, preferred_element_type=jnp.float32
    ).astype(jnp.bfloat16)
    pairwise = jnp.einsum("sfe,sek->sfk", pooled, projected, preferred_element_type=jnp.float32)
    z_local = normalize(pairwise.reshape(samples, -1), ln_gain)

    z_group = gather_nodes(z_local)
    pre_act = jnp.dot(z_group, w_full, preferred_element_type=jnp.float32)
    sigma = jax.nn.sigmoid(pre_act)
    hidden = (pre_act * sigma).astype(jnp.bfloat16)
    d_pre = (d_hidden[0, 0].astype(jnp.float32) * sigma * (1.0 + pre_act * (1.0 - sigma))).astype(
        jnp.bfloat16
    )
    term = lax.dot_general(
        z_group, d_pre, (((0,), (0,)), ((), ())), preferred_element_type=jnp.float32
    ).astype(jnp.bfloat16)
    term = term.reshape(N_X, N_CORE, w_in.shape[0], hidden_here)
    core = lax.axis_index("hst") % N_CORE
    given = lax.dynamic_index_in_dim(term, 1 - core, 1, keepdims=False)
    kept = lax.dynamic_index_in_dim(term, core, 1, keepdims=False)
    pair = add(kept, lax.ppermute(given, "hst", CORE_SWAP)).astype(jnp.bfloat16)
    terms = lax.all_to_all(pair, "hst", 0, 0, axis_index_groups=X_GROUPS, tiled=True)
    share = add(*[terms[i] for i in range(N_X)]).astype(jnp.bfloat16)
    grad_w = add(share, lax.ppermute(share, "dp", DP_SWAP))
    return (hidden.reshape(1, 1, group, hidden_here), grad_w)


def solution(mesh):
    in_specs = (
        P("hst", "dp", "node", None),
        P("dp", "hst", "node", None),
        P(),
        P(),
        P(),
        P("hst", "node"),
        P("dp", "hst", None, "node"),
    )
    out_specs = (P("dp", "hst", None, "node"), P("hst", "node"))
    return jax.shard_map(local, mesh=mesh, in_specs=in_specs, out_specs=out_specs, check_vma=False)
```

```python
import jax
import jax.numpy as jnp
from jax import lax
from jax.experimental import pallas as pl
from jax.experimental.pallas import tpu as pltpu
from jax.sharding import PartitionSpec as P

N_X = 4
N_CORE = 2
N_Y = 8
N_Z = 4
VMEM = 12 * 2**20

def swaps(size, partner):
    return [(i, partner(i)) for i in range(size)]


CORE_SWAP = swaps(N_X * N_CORE, lambda h: h ^ 1)
X_EVEN = swaps(N_X * N_CORE, lambda h: h ^ 2)
X_ODD = swaps(N_X * N_CORE, lambda h: h ^ 6)
Y_EVEN = swaps(N_Y * N_Z, lambda n: n ^ N_Z)
Y_ODD = swaps(N_Y * N_Z, lambda n: (((n // N_Z + 1) ^ 1) - 1) % N_Y * N_Z + n % N_Z)
Z_GROUPS = [[N_Z * y + z for z in range(N_Z)] for y in range(N_Y)]
DP_SWAP = swaps(2, lambda d: d ^ 1)


def add(*terms):
    total = terms[0].astype(jnp.float32)
    for term in terms[1:]:
        total = total + term.astype(jnp.float32)
    return total


def sum_over_x(a, b):
    a_far = lax.ppermute(a[2], "hst", X_EVEN)
    b_far = lax.ppermute(b[2], "hst", X_ODD)
    a_one = lax.ppermute(a[1], "hst", X_EVEN)
    b_one = lax.ppermute(b[3], "hst", X_ODD)
    a_two = lax.ppermute(add(a[3], a_far).astype(a_far.dtype), "hst", X_ODD)
    b_two = lax.ppermute(add(b[1], b_far).astype(b_far.dtype), "hst", X_EVEN)
    return (a[0], a_one, a_two), (b[0], b_one, b_two)


def pack_kernel(h_ref, rows_ref, out_ref, sems):
    rows, samples = rows_ref.shape[0], out_ref.shape[1]
    copies = []
    for j in range(N_X):
        first = pl.multiple_of((h_ref[0] ^ 1 ^ (6 * j % 8)) * samples, samples)
        source = rows_ref.at[:, pl.ds(first, samples)]
        target = out_ref.at[pl.ds(j * rows, rows), :]
        copies.append(pltpu.make_async_copy(source, target, sems.at[j]))
        copies[-1].start()
    for copy in copies:
        copy.wait()


def pair_kernel(h_ref, rows_ref, got_ref, *out_refs):
    total = add(rows_ref[...], got_ref[...]).astype(rows_ref.dtype)
    half = total.shape[0] // 2
    for j in range(N_X):

        @pl.when(pl.program_id(0) == j)
        def _(away=-j % N_X):
            out_refs[away][...] = total[:half]
            out_refs[N_X + away][...] = total[half:]


def turn_kernel(*refs):
    out_ref = refs[-1]
    half = refs[0].shape[0]
    for first, parts in ((0, refs[:3]), (half, refs[3:6])):
        for row in range(0, half, 128):
            total = add(*[part[row : row + 128] for part in parts])
            out_ref[:, first + row : first + row + 128] = total.T.astype(out_ref.dtype)


def sum_partials(flat):
    rows, samples = flat.shape[0], flat.shape[1] // (N_X * N_CORE)
    half = rows // 2
    h = lax.axis_index("hst").astype(jnp.int32).reshape(1)
    params = pltpu.CompilerParams(vmem_limit_bytes=VMEM)
    block = pl.BlockSpec((rows, samples), lambda j, h: (j, 0))
    mine = pl.BlockSpec((rows, samples), lambda j, h: (0, h[0] ^ (6 * j % 8)))
    given = pl.pallas_call(
        pack_kernel,
        out_shape=jax.ShapeDtypeStruct((N_X * rows, samples), flat.dtype),
        grid_spec=pltpu.PrefetchScalarGridSpec(
            num_scalar_prefetch=1,
            grid=(1,),
            in_specs=[pl.BlockSpec(memory_space=pltpu.HBM)],
            out_specs=pl.BlockSpec(memory_space=pl.ANY),
            scratch_shapes=[pltpu.SemaphoreType.DMA((N_X,))],
        ),
        compiler_params=params,
        name="pack",
    )(h, flat)
    got = lax.ppermute(given, "hst", CORE_SWAP)

    out = pl.pallas_call(
        pair_kernel,
        out_shape=[jax.ShapeDtypeStruct((half, samples), flat.dtype)] * (2 * N_X),
        grid_spec=pltpu.PrefetchScalarGridSpec(
            num_scalar_prefetch=1,
            grid=(N_X,),
            in_specs=[mine, block],
            out_specs=[pl.BlockSpec((half, samples), lambda j, h: (0, 0))] * (2 * N_X),
        ),
        compiler_params=params,
        name="pair",
    )(h, flat, got)
    a_parts, b_parts = sum_over_x(out[:N_X], out[N_X:])
    return pl.pallas_call(
        turn_kernel,
        out_shape=jax.ShapeDtypeStruct((samples, rows), flat.dtype),
        compiler_params=params,
        name="turn",
    )(*a_parts, *b_parts)


def normalize(flat_rows, ln_gain):
    middle = jnp.mean(flat_rows, axis=-1, keepdims=True)
    centered = flat_rows - middle
    variance = jnp.mean(centered * centered, axis=-1, keepdims=True)
    return (centered * lax.rsqrt(variance + 1e-05) * ln_gain).astype(jnp.bfloat16)


def gather_nodes(block):
    copies = jnp.broadcast_to(block, (N_Z,) + block.shape)
    line = lax.all_to_all(copies, "node", 0, 0, axis_index_groups=Z_GROUPS, tiled=True)
    line = line.reshape(-1, block.shape[1])
    rows, half = line.shape[0], line.shape[0] // 2
    y = lax.axis_index("node") // N_Z
    sign = 1 - 2 * (y % 2)

    def put(group, part, distance, first_row=0):
        place = (y + sign * distance) % N_Y * rows + first_row
        return lax.dynamic_update_slice(group, part, (place, 0))

    group = put(jnp.zeros((N_Y * rows, line.shape[1]), line.dtype), line, 0)
    pairs = (Y_EVEN, Y_ODD)
    lead = lax.ppermute(line, "node", pairs[0])
    trail = lax.ppermute(line, "node", pairs[1])
    for step in range(1, N_Y // 2):
        pairs = pairs[::-1]
        way = step if step % 2 else -step
        group = put(put(group, lead, way), trail, -way)
        if step == N_Y // 2 - 1:
            lead, trail = lead[half:], trail[:half]
        lead, trail = lax.ppermute(lead, "node", pairs[0]), lax.ppermute(trail, "node", pairs[1])
    return put(put(group, lead, N_Y // 2, half), trail, N_Y // 2)


def local(partials, counts, perm, fm_proj, ln_gain, w_in, d_hidden):
    samples = counts.shape[2]
    group, hidden_here = d_hidden.shape[2], d_hidden.shape[3]
    w_full = lax.all_gather(w_in, "hst", axis=0, tiled=True)
    rows = partials.shape[2] * partials.shape[3]
    summed = sum_partials(partials[0].transpose(1, 2, 0).reshape(rows, -1))
    shard_rows = lax.all_to_all(
        summed.reshape(N_Y * N_Z, samples, rows), "node", split_axis=0, concat_axis=0, tiled=True
    )
    shard_rows = shard_rows.transpose(1, 0, 2).reshape(samples, -1, partials.shape[3])
    ordered = jnp.take(shard_rows, perm, axis=1, mode="clip")
    counts_here = counts[0, 0]
    divisor = jnp.maximum(counts_here, 1).astype(jnp.float32)[:, :, None]
    pooled = jnp.where(
        counts_here[:, :, None] > 0, ordered.astype(jnp.float32) / divisor, 0.0
    ).astype(jnp.bfloat16)
    projected = jnp.einsum(
        "sfe,fk->sek", pooled, fm_proj, preferred_element_type=jnp.float32
    ).astype(jnp.bfloat16)
    pairwise = jnp.einsum("sfe,sek->sfk", pooled, projected, preferred_element_type=jnp.float32)
    z_local = normalize(pairwise.reshape(samples, -1), ln_gain)

    z_group = gather_nodes(z_local)
    pre_act = jnp.dot(z_group, w_full, preferred_element_type=jnp.float32)
    sigma = jax.nn.sigmoid(pre_act)
    hidden = (pre_act * sigma).astype(jnp.bfloat16)
    d_pre = (d_hidden[0, 0].astype(jnp.float32) * sigma * (1.0 + pre_act * (1.0 - sigma))).astype(
        jnp.bfloat16
    )
    term = lax.dot_general(
        z_group, d_pre, (((0,), (0,)), ((), ())), preferred_element_type=jnp.float32
    ).astype(jnp.bfloat16)
    term = term.reshape(N_X, N_CORE, w_in.shape[0], hidden_here)
    core = lax.axis_index("hst") % N_CORE
    given = lax.dynamic_index_in_dim(term, 1 - core, 1, keepdims=False)
    kept = lax.dynamic_index_in_dim(term, core, 1, keepdims=False)
    pair = add(kept, lax.ppermute(given, "hst", CORE_SWAP)).astype(jnp.bfloat16)
    x, half = lax.axis_index("hst") // N_CORE, w_in.shape[0] // 2
    away = [lax.dynamic_index_in_dim(pair, x ^ r, 0, keepdims=False) for r in range(N_X)]
    a, b = [piece[:half] for piece in away], [piece[half:] for piece in away]
    sums = sum_over_x(a, b)
    shares = [add(*parts).astype(jnp.bfloat16) for parts in sums]
    grad_w = [add(share, lax.ppermute(share, "dp", DP_SWAP)) for share in shares]
    grad_w = jnp.concatenate(grad_w, 0)
    return (hidden.reshape(1, 1, group, hidden_here), grad_w)


def solution(mesh):
    in_specs = (
        P("hst", "dp", "node", None),
        P("dp", "hst", "node", None),
        P(),
        P(),
        P(),
        P("hst", "node"),
        P("dp", "hst", None, "node"),
    )
    out_specs = (P("dp", "hst", None, "node"), P("hst", "node"))
    return jax.shard_map(local, mesh=mesh, in_specs=in_specs, out_specs=out_specs, check_vma=False)
```

```python
import jax
import jax.numpy as jnp
from jax import lax
from jax.experimental import pallas as pl
from jax.experimental.pallas import tpu as pltpu
from jax.sharding import PartitionSpec as P

N_X = 4
N_CORE = 2
N_Y = 8
N_Z = 4
VMEM = 12 * 2**20

def swaps(size, partner):
    return [(i, partner(i)) for i in range(size)]


CORE_SWAP = swaps(N_X * N_CORE, lambda h: h ^ 1)
X_EVEN = swaps(N_X * N_CORE, lambda h: h ^ 2)
X_ODD = swaps(N_X * N_CORE, lambda h: h ^ 6)
Y_EVEN = swaps(N_Y * N_Z, lambda n: n ^ N_Z)
Y_ODD = swaps(N_Y * N_Z, lambda n: (((n // N_Z + 1) ^ 1) - 1) % N_Y * N_Z + n % N_Z)
Z_GROUPS = [[N_Z * y + z for z in range(N_Z)] for y in range(N_Y)]
X_GROUPS = [[N_CORE * x + c for x in range(N_X)] for c in range(N_CORE)]
DP_SWAP = swaps(2, lambda d: d ^ 1)


def add(*terms):
    total = terms[0].astype(jnp.float32)
    for term in terms[1:]:
        total = total + term.astype(jnp.float32)
    return total


def pack_kernel(h_ref, rows_ref, out_ref):
    out_ref[...] = rows_ref[...]


def pair_kernel(h_ref, rows_ref, got_ref, *out_refs):
    total = add(rows_ref[...], got_ref[...]).astype(rows_ref.dtype)
    half = total.shape[0] // 2
    for j in range(N_X):

        @pl.when(pl.program_id(0) == j)
        def _(away=-j % N_X):
            out_refs[away][...] = total[:half]
            out_refs[N_X + away][...] = total[half:]


def turn_kernel(*refs):
    out_ref = refs[-1]
    half = refs[0].shape[0]
    for first, parts in ((0, refs[:3]), (half, refs[3:6])):
        for row in range(0, half, 128):
            total = add(*[part[row : row + 128] for part in parts])
            out_ref[:, first + row : first + row + 128] = total.T.astype(out_ref.dtype)


def sum_partials(flat):
    rows, samples = flat.shape[0], flat.shape[1] // (N_X * N_CORE)
    half = rows // 2
    h = lax.axis_index("hst").astype(jnp.int32).reshape(1)
    params = pltpu.CompilerParams(vmem_limit_bytes=VMEM)
    block = pl.BlockSpec((rows, samples), lambda j, h: (j, 0))
    theirs = pl.BlockSpec((rows, samples), lambda j, h: (0, h[0] ^ 1 ^ (6 * j % 8)))
    mine = pl.BlockSpec((rows, samples), lambda j, h: (0, h[0] ^ (6 * j % 8)))
    given = pl.pallas_call(
        pack_kernel,
        out_shape=jax.ShapeDtypeStruct((N_X * rows, samples), flat.dtype),
        grid_spec=pltpu.PrefetchScalarGridSpec(
            num_scalar_prefetch=1, grid=(N_X,), in_specs=[theirs], out_specs=block
        ),
        compiler_params=pltpu.CompilerParams(vmem_limit_bytes=4 * VMEM),
        name="pack",
    )(h, flat)
    got = lax.ppermute(given, "hst", CORE_SWAP)

    out = pl.pallas_call(
        pair_kernel,
        out_shape=[jax.ShapeDtypeStruct((half, samples), flat.dtype)] * (2 * N_X),
        grid_spec=pltpu.PrefetchScalarGridSpec(
            num_scalar_prefetch=1,
            grid=(N_X,),
            in_specs=[mine, block],
            out_specs=[pl.BlockSpec((half, samples), lambda j, h: (0, 0))] * (2 * N_X),
        ),
        compiler_params=params,
        name="pair",
    )(h, flat, got)
    a, b = out[:N_X], out[N_X:]
    a_far = lax.ppermute(a[2], "hst", X_EVEN)
    b_far = lax.ppermute(b[2], "hst", X_ODD)
    a_one = lax.ppermute(a[1], "hst", X_EVEN)
    b_one = lax.ppermute(b[3], "hst", X_ODD)
    a_two = lax.ppermute(add(a[3], a_far).astype(flat.dtype), "hst", X_ODD)
    b_two = lax.ppermute(add(b[1], b_far).astype(flat.dtype), "hst", X_EVEN)
    return pl.pallas_call(
        turn_kernel,
        out_shape=jax.ShapeDtypeStruct((samples, rows), flat.dtype),
        compiler_params=params,
        name="turn",
    )(a[0], a_one, a_two, b[0], b_one, b_two)


def normalize(flat_rows, ln_gain):
    middle = jnp.mean(flat_rows, axis=-1, keepdims=True)
    centered = flat_rows - middle
    variance = jnp.mean(centered * centered, axis=-1, keepdims=True)
    return (centered * lax.rsqrt(variance + 1e-05) * ln_gain).astype(jnp.bfloat16)


def gather_nodes(block, early):
    copies = jnp.broadcast_to(block, (N_Z,) + block.shape)
    line = lax.all_to_all(copies, "node", 0, 0, axis_index_groups=Z_GROUPS, tiled=True)
    line = line.reshape(-1, block.shape[1])
    rows, half = line.shape[0], line.shape[0] // 2
    y = lax.axis_index("node") // N_Z
    sign = 1 - 2 * (y % 2)

    def put(group, part, distance, first_row=0):
        place = (y + sign * distance) % N_Y * rows + first_row
        return lax.dynamic_update_slice(group, part, (place, 0))

    group = put(jnp.zeros((N_Y * rows, line.shape[1]), line.dtype), line, 0)
    pairs = (Y_EVEN, Y_ODD)
    lead = lax.ppermute(line, "node", pairs[0])
    trail = lax.ppermute(line, "node", pairs[1])
    for step in range(1, N_Y // 2):
        pairs = pairs[::-1]
        way = step if step % 2 else -step
        group = put(put(group, lead, way), trail, -way)
        if step == N_Y // 2 - 1:
            trail, early = lax.optimization_barrier((trail, early))
            lead, trail = lead[half:], trail[:half]
        lead, trail = lax.ppermute(lead, "node", pairs[0]), lax.ppermute(trail, "node", pairs[1])
    return put(put(group, lead, N_Y // 2, half), trail, N_Y // 2), early


def local(partials, counts, perm, fm_proj, ln_gain, w_in, d_hidden):
    samples = counts.shape[2]
    group, hidden_here = d_hidden.shape[2], d_hidden.shape[3]
    w_full = lax.all_gather(w_in, "hst", axis=0, tiled=True)
    rows = partials.shape[2] * partials.shape[3]
    summed = sum_partials(partials[0].transpose(1, 2, 0).reshape(rows, -1))
    shard_rows = lax.all_to_all(
        summed.reshape(N_Y * N_Z, samples, rows), "node", split_axis=0, concat_axis=0, tiled=True
    )
    shard_rows = shard_rows.transpose(1, 0, 2).reshape(samples, -1, partials.shape[3])
    ordered = jnp.take(shard_rows, perm, axis=1, mode="clip")
    counts_here = counts[0, 0]
    divisor = jnp.maximum(counts_here, 1).astype(jnp.float32)[:, :, None]
    pooled = jnp.where(
        counts_here[:, :, None] > 0, ordered.astype(jnp.float32) / divisor, 0.0
    ).astype(jnp.bfloat16)
    projected = jnp.einsum(
        "sfe,fk->sek", pooled, fm_proj, preferred_element_type=jnp.float32
    ).astype(jnp.bfloat16)
    pairwise = jnp.einsum("sfe,sek->sfk", pooled, projected, preferred_element_type=jnp.float32)
    z_local = normalize(pairwise.reshape(samples, -1), ln_gain)

    z_group, w_full = gather_nodes(z_local, w_full)
    pre_act = jnp.dot(z_group, w_full, preferred_element_type=jnp.float32)
    sigma = jax.nn.sigmoid(pre_act)
    hidden = (pre_act * sigma).astype(jnp.bfloat16)
    d_pre = (d_hidden[0, 0].astype(jnp.float32) * sigma * (1.0 + pre_act * (1.0 - sigma))).astype(
        jnp.bfloat16
    )
    term = lax.dot_general(
        z_group, d_pre, (((0,), (0,)), ((), ())), preferred_element_type=jnp.float32
    ).astype(jnp.bfloat16)
    term = term.reshape(N_X, N_CORE, w_in.shape[0], hidden_here)
    core = lax.axis_index("hst") % N_CORE
    given = lax.dynamic_index_in_dim(term, 1 - core, 1, keepdims=False)
    kept = lax.dynamic_index_in_dim(term, core, 1, keepdims=False)
    pair = add(kept, lax.ppermute(given, "hst", CORE_SWAP)).astype(jnp.bfloat16)
    terms = lax.all_to_all(pair, "hst", 0, 0, axis_index_groups=X_GROUPS, tiled=True)
    share = add(*[terms[i] for i in range(N_X)]).astype(jnp.bfloat16)
    grad_w = add(share, lax.ppermute(share, "dp", DP_SWAP))
    return (hidden.reshape(1, 1, group, hidden_here), grad_w)


def solution(mesh):
    in_specs = (
        P("hst", "dp", "node", None),
        P("dp", "hst", "node", None),
        P(),
        P(),
        P(),
        P("hst", "node"),
        P("dp", "hst", None, "node"),
    )
    out_specs = (P("dp", "hst", None, "node"), P("hst", "node"))
    return jax.shard_map(local, mesh=mesh, in_specs=in_specs, out_specs=out_specs, check_vma=False)
```

```python
import jax
import jax.numpy as jnp
from jax import lax
from jax.experimental import pallas as pl
from jax.experimental.pallas import tpu as pltpu
from jax.sharding import PartitionSpec as P

N_X = 4
N_CORE = 2
N_Y = 8
N_Z = 4
VMEM = 12 * 2**20

def swaps(size, partner):
    return [(i, partner(i)) for i in range(size)]


CORE_SWAP = swaps(N_X * N_CORE, lambda h: h ^ 1)
X_EVEN = swaps(N_X * N_CORE, lambda h: h ^ 2)
X_ODD = swaps(N_X * N_CORE, lambda h: h ^ 6)
Y_EVEN = swaps(N_Y * N_Z, lambda n: n ^ N_Z)
Y_ODD = swaps(N_Y * N_Z, lambda n: (((n // N_Z + 1) ^ 1) - 1) % N_Y * N_Z + n % N_Z)
Z_SWAPS = [swaps(N_Y * N_Z, lambda n, k=k: n ^ k) for k in range(1, N_Z)]
X_GROUPS = [[N_CORE * x + c for x in range(N_X)] for c in range(N_CORE)]
DP_SWAP = swaps(2, lambda d: d ^ 1)


def add(*terms):
    total = terms[0].astype(jnp.float32)
    for term in terms[1:]:
        total = total + term.astype(jnp.float32)
    return total


def pack_kernel(h_ref, rows_ref, out_ref):
    out_ref[...] = rows_ref[...]


def pair_kernel(h_ref, rows_ref, got_ref, *out_refs):
    total = add(rows_ref[...], got_ref[...]).astype(rows_ref.dtype)
    half = total.shape[0] // 2
    for j in range(N_X):

        @pl.when(pl.program_id(0) == j)
        def _(away=-j % N_X):
            out_refs[away][...] = total[:half]
            out_refs[N_X + away][...] = total[half:]


def turn_kernel(*refs):
    out_ref = refs[-1]
    half = refs[0].shape[0]
    for first, parts in ((0, refs[:3]), (half, refs[3:6])):
        for row in range(0, half, 128):
            total = add(*[part[row : row + 128] for part in parts])
            out_ref[:, first + row : first + row + 128] = total.T.astype(out_ref.dtype)


def sum_partials(flat):
    rows, samples = flat.shape[0], flat.shape[1] // (N_X * N_CORE)
    half = rows // 2
    h = lax.axis_index("hst").astype(jnp.int32).reshape(1)
    params = pltpu.CompilerParams(vmem_limit_bytes=VMEM)
    block = pl.BlockSpec((rows, samples), lambda j, h: (j, 0))
    theirs = pl.BlockSpec((rows, samples), lambda j, h: (0, h[0] ^ 1 ^ (6 * j % 8)))
    mine = pl.BlockSpec((rows, samples), lambda j, h: (0, h[0] ^ (6 * j % 8)))
    given = pl.pallas_call(
        pack_kernel,
        out_shape=jax.ShapeDtypeStruct((N_X * rows, samples), flat.dtype),
        grid_spec=pltpu.PrefetchScalarGridSpec(
            num_scalar_prefetch=1, grid=(N_X,), in_specs=[theirs], out_specs=block
        ),
        compiler_params=pltpu.CompilerParams(vmem_limit_bytes=4 * VMEM),
        name="pack",
    )(h, flat)
    got = lax.ppermute(given, "hst", CORE_SWAP)

    out = pl.pallas_call(
        pair_kernel,
        out_shape=[jax.ShapeDtypeStruct((half, samples), flat.dtype)] * (2 * N_X),
        grid_spec=pltpu.PrefetchScalarGridSpec(
            num_scalar_prefetch=1,
            grid=(N_X,),
            in_specs=[mine, block],
            out_specs=[pl.BlockSpec((half, samples), lambda j, h: (0, 0))] * (2 * N_X),
        ),
        compiler_params=params,
        name="pair",
    )(h, flat, got)
    a, b = out[:N_X], out[N_X:]
    a_far = lax.ppermute(a[2], "hst", X_EVEN)
    b_far = lax.ppermute(b[2], "hst", X_ODD)
    a_one = lax.ppermute(a[1], "hst", X_EVEN)
    b_one = lax.ppermute(b[3], "hst", X_ODD)
    a_two = lax.ppermute(add(a[3], a_far).astype(flat.dtype), "hst", X_ODD)
    b_two = lax.ppermute(add(b[1], b_far).astype(flat.dtype), "hst", X_EVEN)
    return pl.pallas_call(
        turn_kernel,
        out_shape=jax.ShapeDtypeStruct((samples, rows), flat.dtype),
        compiler_params=params,
        name="turn",
    )(a[0], a_one, a_two, b[0], b_one, b_two)


def normalize(flat_rows, ln_gain):
    middle = jnp.mean(flat_rows, axis=-1, keepdims=True)
    centered = flat_rows - middle
    variance = jnp.mean(centered * centered, axis=-1, keepdims=True)
    return (centered * lax.rsqrt(variance + 1e-05) * ln_gain).astype(jnp.bfloat16)


def gather_nodes(block):
    z, samples = lax.axis_index("node") % N_Z, block.shape[0]
    line = jnp.zeros((N_Z * samples, block.shape[1]), block.dtype)
    near = [lax.ppermute(block, "node", pairs) for pairs in Z_SWAPS]
    for other, part in enumerate([block] + near):
        line = lax.dynamic_update_slice(line, part, ((z ^ other) * samples, 0))
    rows, half = line.shape[0], line.shape[0] // 2
    y = lax.axis_index("node") // N_Z
    sign = 1 - 2 * (y % 2)

    def put(group, part, distance, first_row=0):
        place = (y + sign * distance) % N_Y * rows + first_row
        return lax.dynamic_update_slice(group, part, (place, 0))

    group = put(jnp.zeros((N_Y * rows, line.shape[1]), line.dtype), line, 0)
    pairs = (Y_EVEN, Y_ODD)
    lead = lax.ppermute(line, "node", pairs[0])
    trail = lax.ppermute(line, "node", pairs[1])
    for step in range(1, N_Y // 2):
        pairs = pairs[::-1]
        way = step if step % 2 else -step
        group = put(put(group, lead, way), trail, -way)
        if step == N_Y // 2 - 1:
            lead, trail = lead[half:], trail[:half]
        lead, trail = lax.ppermute(lead, "node", pairs[0]), lax.ppermute(trail, "node", pairs[1])
    return put(put(group, lead, N_Y // 2, half), trail, N_Y // 2)


def local(partials, counts, perm, fm_proj, ln_gain, w_in, d_hidden):
    samples = counts.shape[2]
    group, hidden_here = d_hidden.shape[2], d_hidden.shape[3]
    w_full = lax.all_gather(w_in, "hst", axis=0, tiled=True)
    rows = partials.shape[2] * partials.shape[3]
    summed = sum_partials(partials[0].transpose(1, 2, 0).reshape(rows, -1))
    shard_rows = lax.all_to_all(
        summed.reshape(N_Y * N_Z, samples, rows), "node", split_axis=0, concat_axis=0, tiled=True
    )
    shard_rows = shard_rows.transpose(1, 0, 2).reshape(samples, -1, partials.shape[3])
    ordered = jnp.take(shard_rows, perm, axis=1, mode="clip")
    counts_here = counts[0, 0]
    divisor = jnp.maximum(counts_here, 1).astype(jnp.float32)[:, :, None]
    pooled = jnp.where(
        counts_here[:, :, None] > 0, ordered.astype(jnp.float32) / divisor, 0.0
    ).astype(jnp.bfloat16)
    projected = jnp.einsum(
        "sfe,fk->sek", pooled, fm_proj, preferred_element_type=jnp.float32
    ).astype(jnp.bfloat16)
    pairwise = jnp.einsum("sfe,sek->sfk", pooled, projected, preferred_element_type=jnp.float32)
    z_local = normalize(pairwise.reshape(samples, -1), ln_gain)

    z_group = gather_nodes(z_local)
    pre_act = jnp.dot(z_group, w_full, preferred_element_type=jnp.float32)
    sigma = jax.nn.sigmoid(pre_act)
    hidden = (pre_act * sigma).astype(jnp.bfloat16)
    d_pre = (d_hidden[0, 0].astype(jnp.float32) * sigma * (1.0 + pre_act * (1.0 - sigma))).astype(
        jnp.bfloat16
    )
    term = lax.dot_general(
        z_group, d_pre, (((0,), (0,)), ((), ())), preferred_element_type=jnp.float32
    ).astype(jnp.bfloat16)
    term = term.reshape(N_X, N_CORE, w_in.shape[0], hidden_here)
    core = lax.axis_index("hst") % N_CORE
    given = lax.dynamic_index_in_dim(term, 1 - core, 1, keepdims=False)
    kept = lax.dynamic_index_in_dim(term, core, 1, keepdims=False)
    pair = add(kept, lax.ppermute(given, "hst", CORE_SWAP)).astype(jnp.bfloat16)
    terms = lax.all_to_all(pair, "hst", 0, 0, axis_index_groups=X_GROUPS, tiled=True)
    share = add(*[terms[i] for i in range(N_X)]).astype(jnp.bfloat16)
    grad_w = add(share, lax.ppermute(share, "dp", DP_SWAP))
    return (hidden.reshape(1, 1, group, hidden_here), grad_w)


def solution(mesh):
    in_specs = (
        P("hst", "dp", "node", None),
        P("dp", "hst", "node", None),
        P(),
        P(),
        P(),
        P("hst", "node"),
        P("dp", "hst", None, "node"),
    )
    out_specs = (P("dp", "hst", None, "node"), P("hst", "node"))
    return jax.shard_map(local, mesh=mesh, in_specs=in_specs, out_specs=out_specs, check_vma=False)
```
